32 devices in a mesh: groups: 1, gy: 8 (over z, y), gx: 4 (over x, core).
Axes of the slice: x: 2, y: 2, z: 4, core: 2. Of those that a mesh axis runs over, the one named last changes fastest.
Arguments:
- features: bfloat16 [64, 128, 128], P(('groups', 'gy'), 'gx'), may hold values from -6 to 6
- scene_codes: int32 [64, 128], P(('groups', 'gy'), 'gx'), may hold values from 0 to 255
- norm_gain: float32 [128], replicated, may hold values from 0.5 to 1.5
- in_weight: bfloat16 [128, 512], replicated, may hold values from -0.5 to 0.5
- conv_weight: float32 [3, 3, 256], replicated, may hold values from -2 to 2
- conv_bias: float32 [256], replicated, may hold values from -3 to 3
- proj_weight: bfloat16 [256, 160], replicated, may hold values from -0.375 to 0.375
- step_weight: float32 [4, 8, 256], replicated, may hold values from -2 to 2
- step_bias: float32 [4, 256], replicated, may hold values from -0.5 to 0.5
- code_table: float32 [256, 256], replicated, may hold values from -1.5 to 86.4
- decay_rates: float32 [4, 16, 256], replicated, may hold values from 0 to 0.15, as said below
- skip_gain: float32 [4, 256], replicated, may hold values from 0.5 to 1.5
- out_gain: float32 [256], replicated, may hold values from 0.5 to 1.5
- out_weight: bfloat16 [256, 128], replicated, may hold values from -0.375 to 0.375
Outputs:
- block_out: bfloat16 [64, 128, 128], P(('groups', 'gy'), 'gx')
The draws below stay inside these ranges and needn't reach their ends.
Inputs may be any that keep to these rules, and one draw needn't show every extreme that they name: `decay_rates`: positive rates.
All inputs are finite; a program needn't handle non-finite values.
Results may differ from the reference program's by a relative error of at most 0.0075.
Values may be sent and summed in bfloat16 or wider, within the bound.
A program may use at most 128 MiB of HBM per device.

```python
import jax
import jax.numpy as jnp
from jax import lax

C = 128
INNER_SIZE = 256
N = 16
R = 8
PATCH_CODES = 256
H = 64
W = 128


def draw_code_table(key, part):
    row_keys, gentle_key, spike_key = jax.random.split(jax.random.fold_in(key, 11), 3)
    spike_rows = jax.random.randint(row_keys, (PATCH_CODES, 1), 0, 64) == 0
    gentle_level = jax.random.uniform(gentle_key, (PATCH_CODES, INNER_SIZE), jnp.float32, -1.0, 1.0)
    extent_reach = (H + W) / 2.0
    sharp_spike = extent_reach * jax.random.uniform(spike_key, (PATCH_CODES, INNER_SIZE), jnp.float32, 0.3, 0.9)
    return jnp.where(spike_rows, sharp_spike, gentle_level).astype(jnp.float32)


def draw_decay_rates(key, part):
    key_pick, key_slow, key_fast = jax.random.split(jax.random.fold_in(key, 23), 3)
    share = 0.5
    slow_pick = jax.random.uniform(key_pick, (4, 1, INNER_SIZE), jnp.float32) < share
    lengths = jnp.array([W, W, H, H], jnp.float32).reshape(4, 1, 1)
    slow = jax.random.uniform(key_slow, (4, N, INNER_SIZE), jnp.float32, 0.4, 1.0) / lengths
    fast = jax.random.uniform(key_fast, (4, N, INNER_SIZE), jnp.float32, 0.05, 0.15)
    return jnp.where(slow_pick, slow, fast).astype(jnp.float32)


def touch_ends(values, own_key, least, high):
    index_at = [jax.random.randint(jax.random.fold_in(own_key, axis), (), 0, length) for axis, length in enumerate(values.shape)]
    widest = values.shape.index(max(values.shape))
    neighbour = index_at[:widest] + [(index_at[widest] + 1) % values.shape[widest]] + index_at[widest + 1:]
    return values.at[tuple(index_at)].set(least).at[tuple(neighbour)].set(high)


def block_levels(stream_key, extent, shards, smallest, top_value):
    def one(axis_at, blocks):
        steps = jax.random.uniform(jax.random.fold_in(jax.random.fold_in(stream_key, 6), axis_at), (blocks,), jnp.float32, smallest / len(shards), top_value / len(shards))
        return jnp.repeat(jnp.exp(steps), extent[axis_at] // blocks).reshape((-1,) + (1,) * (len(extent) - axis_at - 1))

    factor_of = one(*shards[0])
    for cut in shards[1:]:
        factor_of = factor_of * one(*cut)
    return factor_of


def normal_values(stream_key, extent, width, most, shards=(), dtype=jnp.bfloat16):
    level = block_levels(stream_key, extent, shards, -0.22, 0.18) if shards else 1.0
    result = jax.random.normal(stream_key, extent, jnp.float32) * width * level
    return jnp.minimum(jnp.maximum(result, -most), most).astype(dtype)


def setup_inputs(seed: int = 0, part: int = 0) -> dict:
    streams_of = jax.random.split(jax.random.key(seed), 15)
    part_splits = jax.random.split(jax.random.fold_in(streams_of[14], part), 15)
    features = normal_values(part_splits[0], (H, W, C), 1.0, 6.0, ((0, 8), (1, 4)))
    scene_codes = touch_ends(jax.random.randint(part_splits[1], (H, W), 0, PATCH_CODES), jax.random.fold_in(part_splits[1], 1), 0, PATCH_CODES - 1).astype(jnp.int32)
    norm_gain = jnp.clip(1.0 + 0.1 * jax.random.normal(streams_of[2], (C,), jnp.float32), 0.5, 1.5)
    in_weight = normal_values(streams_of[3], (C, 2 * INNER_SIZE), C ** -0.5, 0.5)
    conv_weight = normal_values(streams_of[4], (3, 3, INNER_SIZE), 9 ** -0.5, 2.0, (), jnp.float32)
    conv_bias = normal_values(streams_of[5], (INNER_SIZE,), 0.5, 3.0, (), jnp.float32)
    proj_weight = normal_values(streams_of[6], (INNER_SIZE, 4 * (R + 2 * N)), INNER_SIZE ** -0.5, 0.375)
    step_weight = normal_values(streams_of[7], (4, R, INNER_SIZE), R ** -0.5, 2.0, (), jnp.float32)
    step_bias = jnp.clip(jax.random.uniform(streams_of[8], (4, INNER_SIZE), jnp.float32, -0.5, 0.5), -0.5, 0.5)
    code_table = draw_code_table(jax.random.fold_in(streams_of[14], 71), part)
    decay_rates = draw_decay_rates(jax.random.fold_in(streams_of[14], 71), part)
    skip_gain = jnp.clip(jax.random.uniform(streams_of[11], (4, INNER_SIZE), jnp.float32, 0.5, 1.5), 0.5, 1.5)
    out_gain = jnp.clip(1.0 + 0.1 * jax.random.normal(streams_of[12], (INNER_SIZE,), jnp.float32), 0.5, 1.5)
    out_weight = normal_values(streams_of[13], (INNER_SIZE, C), INNER_SIZE ** -0.5, 0.375)
    return dict(features=features, scene_codes=scene_codes, norm_gain=norm_gain, in_weight=in_weight, conv_weight=conv_weight, conv_bias=conv_bias, proj_weight=proj_weight, step_weight=step_weight, step_bias=step_bias, code_table=code_table, decay_rates=decay_rates, skip_gain=skip_gain, out_gain=out_gain, out_weight=out_weight)


def layer_norm(values, gain):
    mean = lax.optimization_barrier(jnp.mean(values, axis=-1, keepdims=True))
    centered = values - mean
    spread = lax.optimization_barrier(jnp.mean(centered * centered, axis=-1, keepdims=True))
    return centered * lax.rsqrt(spread + 1e-05) * gain

def path_scan(step_size, in_coef, out_coef, signal, rates, reverse):
    line_count = step_size.shape[1]

    def advance(state, inputs):
        sizes, coefs_in, coefs_out, values = inputs
        decays = jnp.exp(-sizes[:, None, :] * rates[None])
        state = decays * state + sizes[:, None, :] * coefs_in[:, :, None] * values[:, None, :]
        return (state, lax.optimization_barrier(jnp.sum(coefs_out[:, :, None] * state, axis=1)))
    start = jnp.zeros((line_count, rates.shape[0], rates.shape[1]), jnp.float32)
    _, outputs = lax.scan(advance, start, (step_size, in_coef, out_coef, signal), reverse=reverse)
    return outputs

def reference(features, scene_codes, norm_gain, in_weight, conv_weight, conv_bias, proj_weight, step_weight, step_bias, code_table, decay_rates, skip_gain, out_gain, out_weight):
    source = features.astype(jnp.float32)
    normed = layer_norm(source, norm_gain).astype(jnp.bfloat16)
    projected = jnp.dot(normed.reshape(H * W, C), in_weight, preferred_element_type=jnp.float32).reshape(H, W, 2 * INNER_SIZE)
    inner = projected[:, :, :INNER_SIZE].astype(jnp.bfloat16)
    gate = projected[:, :, INNER_SIZE:].astype(jnp.bfloat16)
    padded = jnp.pad(inner.astype(jnp.float32), ((1, 1), (1, 1), (0, 0)))
    summed = jnp.zeros((H, W, INNER_SIZE), jnp.float32) + conv_bias
    for row_off in range(3):
        for col_off in range(3):
            summed = summed + padded[row_off:row_off + H, col_off:col_off + W] * conv_weight[row_off, col_off]
    signal_low = jax.nn.silu(summed).astype(jnp.bfloat16)
    signal = signal_low.astype(jnp.float32)
    coefs = jnp.dot(signal_low.reshape(H * W, INNER_SIZE), proj_weight, preferred_element_type=jnp.float32).reshape(H, W, 4, R + 2 * N)
    code_add = code_table[scene_codes]
    total = jnp.zeros((H, W, INNER_SIZE), jnp.float32)
    for direction in range(4):
        piece = coefs[:, :, direction, :]
        low_part = piece[:, :, :R]
        in_coef = piece[:, :, R:R + N]
        out_coef = piece[:, :, R + N:]
        step_size = jax.nn.softplus(jnp.einsum('hwr,re->hwe', low_part, step_weight[direction], precision=lax.Precision.HIGHEST) + step_bias[direction] + code_add)
        arrays = (step_size, in_coef, out_coef, signal)
        if direction < 2:
            arrays = tuple((jnp.swapaxes(value, 0, 1) for value in arrays))
        outputs = path_scan(arrays[0], arrays[1], arrays[2], arrays[3], decay_rates[direction], direction % 2 == 1)
        if direction < 2:
            outputs = jnp.swapaxes(outputs, 0, 1)
        total = total + outputs + skip_gain[direction] * signal
    normed_out = layer_norm(total, out_gain)
    mixed = (normed_out * jax.nn.silu(gate.astype(jnp.float32))).astype(jnp.bfloat16)
    added = jnp.dot(mixed.reshape(H * W, INNER_SIZE), out_weight, preferred_element_type=jnp.float32).reshape(H, W, C)
    return (source + added).astype(jnp.bfloat16)
```

```python
import functools
import math

import jax
import jax.numpy as jnp
from jax import lax
from jax.experimental import pallas as pl
from jax.experimental.pallas import tpu as pltpu
from jax.sharding import PartitionSpec as P

MESH = pl.DeviceIdType.MESH
LANES = 128


def layer_norm(values, gain):
    mean = jnp.mean(values, axis=-1, keepdims=True)
    centered = values - mean
    spread = jnp.mean(centered * centered, axis=-1, keepdims=True)
    return centered * lax.rsqrt(spread + 1e-05) * gain


def exchange_kernel(nx, ny, xr, xc, out_r, out_c, send_r, recv_r, send_c, recv_c, own_sem):
    group = lax.axis_index("groups")
    row = lax.axis_index("gy")
    col = lax.axis_index("gx")
    barrier = pltpu.get_barrier_semaphore()
    for k in range(1, nx):
        pl.semaphore_signal(
            barrier, inc=1, device_id=(group, row, lax.rem(col + k, nx)), device_id_type=MESH
        )
    for k in range(1, ny):
        pl.semaphore_signal(
            barrier, inc=1, device_id=(group, lax.rem(row + k, ny), col), device_id_type=MESH
        )
    own_r = pltpu.make_async_copy(xr.at[col], out_r.at[col], own_sem.at[0])
    own_c = pltpu.make_async_copy(xc.at[row], out_c.at[row], own_sem.at[1])
    own_r.start()
    own_c.start()
    pl.semaphore_wait(barrier, nx + ny - 2)
    copies = []
    for k in range(1, ny):
        to = lax.rem(row + k, ny)
        copies.append(
            pltpu.make_async_remote_copy(
                src_ref=xc.at[to],
                dst_ref=out_c.at[row],
                send_sem=send_c.at[k - 1],
                recv_sem=recv_c.at[k - 1],
                device_id=(group, to, col),
                device_id_type=MESH,
            )
        )
        copies[-1].start()
    for k in range(1, nx):
        to = lax.rem(col + k, nx)
        copies.append(
            pltpu.make_async_remote_copy(
                src_ref=xr.at[to],
                dst_ref=out_r.at[col],
                send_sem=send_r.at[k - 1],
                recv_sem=recv_r.at[k - 1],
                device_id=(group, row, to),
                device_id_type=MESH,
            )
        )
        copies[-1].start()
    own_r.wait()
    own_c.wait()
    for copy in copies:
        copy.wait()


def exchange(xr, xc, call):
    nx, ny = xr.shape[0], xc.shape[0]
    return pl.pallas_call(
        functools.partial(exchange_kernel, nx, ny),
        out_shape=(
            jax.ShapeDtypeStruct(xr.shape, xr.dtype),
            jax.ShapeDtypeStruct(xc.shape, xc.dtype),
        ),
        in_specs=[pl.BlockSpec(memory_space=pltpu.VMEM)] * 2,
        out_specs=(pl.BlockSpec(memory_space=pltpu.VMEM),) * 2,
        scratch_shapes=[
            pltpu.SemaphoreType.DMA((nx - 1,)),
            pltpu.SemaphoreType.DMA((nx - 1,)),
            pltpu.SemaphoreType.DMA((ny - 1,)),
            pltpu.SemaphoreType.DMA((ny - 1,)),
            pltpu.SemaphoreType.DMA((2,)),
        ],
        compiler_params=pltpu.CompilerParams(
            collective_id=call, has_side_effects=True, vmem_limit_bytes=16 * 2**20
        ),
    )(xr, xc)


def scan_kernel(states, step_r, drive_r, coef_r, rate_r, step_c, drive_c, coef_c, rate_c, y_r, y_c):
    def run(step, drive, coef, rate, out):
        length, lines = step.shape[0], step.shape[1]

        def advance(t, state):
            size, push, mix = step[t], drive[t], coef[t]
            new = []
            parts = [None] * 4
            for n in range(states):
                decay = jnp.exp2(size * rate[n])
                now = decay * state[n] + push * mix[:, n : n + 1]
                new.append(now)
                term = now * mix[:, states + n : states + n + 1]
                parts[n % 4] = term if parts[n % 4] is None else parts[n % 4] + term
            out[t] = (parts[0] + parts[1]) + (parts[2] + parts[3])
            return tuple(new)

        start = tuple(jnp.zeros((lines, LANES), jnp.float32) for _ in range(states))
        lax.fori_loop(0, length, advance, start, unroll=2)

    run(step_r, drive_r, coef_r, rate_r, y_r)
    run(step_c, drive_c, coef_c, rate_c, y_c)


def scans(row_args, col_args, states):
    return pl.pallas_call(
        functools.partial(scan_kernel, states),
        out_shape=(
            jax.ShapeDtypeStruct(row_args[0].shape, jnp.float32),
            jax.ShapeDtypeStruct(col_args[0].shape, jnp.float32),
        ),
        in_specs=[pl.BlockSpec(memory_space=pltpu.VMEM)] * 8,
        out_specs=(pl.BlockSpec(memory_space=pltpu.VMEM),) * 2,
        compiler_params=pltpu.CompilerParams(vmem_limit_bytes=32 * 2**20),
    )(*row_args, *col_args)


def fold(values):
    _, lines, length, channels = values.shape
    halves = channels // LANES
    flipped = jnp.stack([values[0], jnp.flip(values[1], 1)])
    split = flipped.reshape(2, lines, length, halves, LANES)
    return split.transpose(2, 3, 0, 1, 4).reshape(length, halves * 2 * lines, LANES)


def strip_inputs(feats, codes, conv, weights, first):
    (norm_gain, in_weight, conv_bias, proj_weight, step_weight, step_bias, code_table, decay_rates) = weights
    lines, length = codes.shape
    inner_width = in_weight.shape[1] // 2
    states, low_rank = decay_rates.shape[1], step_weight.shape[1]
    halves = inner_width // LANES
    wide = low_rank + 2 * states
    normed = layer_norm(feats.astype(jnp.float32), norm_gain).astype(jnp.bfloat16)
    inner = jnp.dot(
        normed.reshape(-1, feats.shape[2]),
        in_weight[:, :inner_width],
        preferred_element_type=jnp.float32,
    ).astype(jnp.bfloat16)
    inner = inner.reshape(lines + 2, length, inner_width)
    padded = jnp.pad(inner, ((0, 0), (1, 1), (0, 0)))
    summed = jnp.zeros((lines, length, inner_width), jnp.float32) + conv_bias
    for a in range(3):
        for b in range(3):
            summed = (
                summed + padded[a : a + lines, b : b + length].astype(jnp.float32) * conv[a, b]
            )
    signal_low = jax.nn.silu(summed).astype(jnp.bfloat16)
    signal = signal_low.astype(jnp.float32)
    coefs = jnp.dot(
        signal_low.reshape(-1, inner_width),
        proj_weight[:, first * wide : (first + 2) * wide],
        preferred_element_type=jnp.float32,
    ).reshape(lines, length, 2, wide)
    one_hot = (codes[:, :, None] == jnp.arange(code_table.shape[0])).astype(jnp.float32)
    offsets = jnp.einsum("pqk,ke->pqe", one_hot, code_table, precision=lax.Precision.HIGHEST)
    step = jax.nn.softplus(
        jnp.einsum(
            "pqdr,dre->dpqe",
            coefs[..., :low_rank],
            step_weight[first : first + 2],
            precision=lax.Precision.HIGHEST,
        )
        + step_bias[first : first + 2, None, None, :]
        + offsets
    )
    mix = coefs[..., low_rank:].transpose(2, 0, 1, 3)
    mix = jnp.stack([mix[0], jnp.flip(mix[1], 1)]).transpose(2, 0, 1, 3)
    mix = mix.reshape(length, 1, 2 * lines, 2 * states)
    mix = jnp.broadcast_to(mix, (length, halves, 2 * lines, 2 * states))
    mix = mix.reshape(length, halves * 2 * lines, 2 * states)
    rate = (decay_rates[first : first + 2] * (-1.0 / math.log(2.0))).reshape(2, states, halves, LANES)
    rate = jnp.broadcast_to(
        rate.transpose(1, 2, 0, 3)[:, :, :, None, :], (states, halves, 2, lines, LANES)
    ).reshape(states, halves * 2 * lines, LANES)
    return (fold(step), fold(step * signal), mix, rate), signal


def unfold(y, lines, channels):
    length = y.shape[0]
    y = y.reshape(length, channels // LANES, 2, lines, LANES)
    y = y[:, :, 0] + jnp.flip(y[:, :, 1], 0)
    return y.transpose(2, 0, 1, 3).reshape(lines, length, channels)


def shifted(part, axis, up):
    count = lax.axis_size(axis)
    pairs = [(i, i + 1) if up else (i + 1, i) for i in range(count - 1)]
    return lax.ppermute(part, axis, pairs)


def on_device(
    features,
    scene_codes,
    norm_gain,
    in_weight,
    conv_weight,
    conv_bias,
    proj_weight,
    step_weight,
    step_bias,
    code_table,
    decay_rates,
    skip_gain,
    out_gain,
    out_weight,
):
    nx, ny = lax.axis_size("gx"), lax.axis_size("gy")
    rows, cols, width = features.shape
    inner_width = in_weight.shape[1] // 2
    states = decay_rates.shape[1]
    rp, cp = rows // nx, cols // ny
    codes = scene_codes.astype(jnp.bfloat16)

    def payload(block, code):
        lines, length, _ = block.shape
        size = -(-(length + 1) // 16) * 16
        code = jnp.pad(code[:, None, :], ((0, 0), (0, size - length - 1), (0, width - length)))
        return jnp.concatenate([block, code], axis=1)

    row_load = payload(features, codes)
    col_load = payload(jnp.swapaxes(features, 0, 1), codes.T)
    row_size, col_size = row_load.shape[1], col_load.shape[1]
    row_load = jnp.concatenate(
        [shifted(row_load[-1:], "gy", True), row_load, shifted(row_load[:1], "gy", False)]
    )
    col_load = jnp.concatenate(
        [shifted(col_load[-1:], "gx", True), col_load, shifted(col_load[:1], "gx", False)]
    )
    xr = jnp.stack([row_load[k * rp : k * rp + rp + 2] for k in range(nx)])
    xc = jnp.stack([col_load[k * cp : k * cp + cp + 2] for k in range(ny)])
    got_r, got_c = exchange(
        xr.reshape(nx, (rp + 2) * row_size, width), xc.reshape(ny, (cp + 2) * col_size, width), 0
    )

    def assembled(got, parts, lines, size, length):
        got = got.reshape(parts, lines + 2, size, width).transpose(1, 0, 2, 3)
        feats = got[:, :, :length].reshape(lines + 2, parts * length, width)
        code = got[1:-1, :, length, :length].reshape(lines, parts * length)
        return feats, code.astype(jnp.int32)

    weights = (
        norm_gain, in_weight, conv_bias, proj_weight, step_weight, step_bias, code_table, decay_rates,
    )
    feats_r, codes_r = assembled(got_r, nx, rp, row_size, cols)
    feats_c, codes_c = assembled(got_c, ny, cp, col_size, rows)
    row_args, signal_r = strip_inputs(feats_r, codes_r, conv_weight, weights, 0)
    col_args, signal_c = strip_inputs(feats_c, codes_c, jnp.swapaxes(conv_weight, 0, 1), weights, 2)
    y_r, y_c = scans(row_args, col_args, states)
    y_r = unfold(y_r, rp, inner_width) + (skip_gain[0] + skip_gain[1]) * signal_r
    y_c = unfold(y_c, cp, inner_width) + (skip_gain[2] + skip_gain[3]) * signal_c
    y_r = y_r.astype(jnp.bfloat16).reshape(rp, nx, cols, inner_width).transpose(1, 0, 2, 3)
    y_c = y_c.astype(jnp.bfloat16).reshape(cp, ny, rows, inner_width).transpose(1, 0, 2, 3)
    back_r, back_c = exchange(
        y_r.reshape(nx, rp * cols, inner_width), y_c.reshape(ny, cp * rows, inner_width), 1
    )
    back_r = back_r.astype(jnp.float32).reshape(rows, cols, inner_width)
    back_c = back_c.astype(jnp.float32).reshape(cols, rows, inner_width)
    total = back_r + jnp.swapaxes(back_c, 0, 1)

    source = features.astype(jnp.float32)
    normed = layer_norm(source, norm_gain).astype(jnp.bfloat16)
    gate = jnp.dot(
        normed.reshape(-1, width), in_weight[:, inner_width:], preferred_element_type=jnp.float32
    ).astype(jnp.bfloat16).reshape(rows, cols, inner_width)
    normed_out = layer_norm(total, out_gain)
    mixed = (normed_out * jax.nn.silu(gate.astype(jnp.float32))).astype(jnp.bfloat16)
    added = jnp.dot(
        mixed.reshape(-1, inner_width), out_weight, preferred_element_type=jnp.float32
    ).reshape(rows, cols, width)
    return (source + added).astype(jnp.bfloat16)


def solution(mesh):
    placed = (P(("groups", "gy"), "gx", None), P(("groups", "gy"), "gx")) + (P(),) * 12
    return jax.shard_map(
        on_device,
        mesh=mesh,
        in_specs=placed,
        out_specs=P(("groups", "gy"), "gx", None),
        check_vma=False,
    )
```

```python
import functools
import math

import jax
import jax.numpy as jnp
from jax import lax
from jax.experimental import pallas as pl
from jax.experimental.pallas import tpu as pltpu
from jax.sharding import PartitionSpec as P

MESH = pl.DeviceIdType.MESH
LANES = 128


def layer_norm(values, gain):
    mean = jnp.mean(values, axis=-1, keepdims=True)
    centered = values - mean
    spread = jnp.mean(centered * centered, axis=-1, keepdims=True)
    return centered * lax.rsqrt(spread + 1e-05) * gain


def exchange_kernel(nx, ny, halo, *refs):
    refs = list(refs)
    take = lambda count: [refs.pop(0) for _ in range(count)]
    xr, xc = take(2)
    edge_r, edge_c = take(2) if halo else (None, None)
    out_r, out_c = take(2)
    halo_r, halo_c = take(2) if halo else (None, None)
    send_r, recv_r, send_c, recv_c, own_sem = take(5)
    edge_sem, halo_r_sem, halo_c_sem = take(3) if halo else (None,) * 3
    group = lax.axis_index("groups")
    row = lax.axis_index("gy")
    col = lax.axis_index("gx")
    barrier = pltpu.get_barrier_semaphore()
    inside_up, inside_down = row > 0, row < ny - 1
    inside_left, inside_right = col > 0, col < nx - 1

    def greet(to_row, to_col):
        pl.semaphore_signal(barrier, inc=1, device_id=(group, to_row, to_col), device_id_type=MESH)

    for k in range(1, nx):
        greet(row, lax.rem(col + k, nx))
    for k in range(1, ny):
        greet(lax.rem(row + k, ny), col)
    if halo:
        receives = (
            (inside_up & (col == 0), [(lax.rem(row + ny - 1, ny), s) for s in range(nx)]),
            (inside_down & (col == nx - 1), [(lax.rem(row + 1, ny), s) for s in range(nx)]),
            (inside_left & (row == 0), [(s, lax.rem(col + nx - 1, nx)) for s in range(ny)]),
            (inside_right & (row == ny - 1), [(s, lax.rem(col + 1, nx)) for s in range(ny)]),
        )
        for here, sources in receives:

            @pl.when(here)
            def _(sources=sources):
                for source in sources:
                    greet(*source)

    own_r = pltpu.make_async_copy(xr.at[col], out_r.at[col], own_sem.at[0])
    own_c = pltpu.make_async_copy(xc.at[row], out_c.at[row], own_sem.at[1])
    own_r.start()
    own_c.start()
    peers = nx + ny - 2
    if halo:
        peers += lax.div(row + ny - 1, ny) + 1 - lax.div(row + 1, ny)
        peers += lax.div(col + nx - 1, nx) + 1 - lax.div(col + 1, nx)
    pl.semaphore_wait(barrier, peers)
    copies = []
    if halo:
        def edge(which, slot):
            down = which % 2 == 0
            if which < 2:
                return pltpu.make_async_remote_copy(
                    src_ref=edge_r.at[1 if down else 0],
                    dst_ref=halo_r.at[which * nx + slot],
                    send_sem=edge_sem.at[which],
                    recv_sem=halo_r_sem.at[which * nx + slot],
                    device_id=(group, lax.rem(row + (1 if down else ny - 1), ny), 0 if down else nx - 1),
                    device_id_type=MESH,
                )
            return pltpu.make_async_remote_copy(
                src_ref=edge_c.at[1 if down else 0],
                dst_ref=halo_c.at[(which - 2) * ny + slot],
                send_sem=edge_sem.at[which],
                recv_sem=halo_c_sem.at[(which - 2) * ny + slot],
                device_id=(group, 0 if down else ny - 1, lax.rem(col + (1 if down else nx - 1), nx)),
                device_id_type=MESH,
            )

        sends = (inside_down, inside_up, inside_right, inside_left)
        for which in range(4):

            @pl.when(sends[which])
            def _(which=which):
                edge(which, col if which < 2 else row).start()

    for k in range(1, ny):
        to = lax.rem(row + k, ny)
        copies.append(
            pltpu.make_async_remote_copy(
                src_ref=xc.at[to],
                dst_ref=out_c.at[row],
                send_sem=send_c.at[k - 1],
                recv_sem=recv_c.at[k - 1],
                device_id=(group, to, col),
                device_id_type=MESH,
            )
        )
        copies[-1].start()
    for k in range(1, nx):
        to = lax.rem(col + k, nx)
        copies.append(
            pltpu.make_async_remote_copy(
                src_ref=xr.at[to],
                dst_ref=out_r.at[col],
                send_sem=send_r.at[k - 1],
                recv_sem=recv_r.at[k - 1],
                device_id=(group, row, to),
                device_id_type=MESH,
            )
        )
        copies[-1].start()
    own_r.wait()
    own_c.wait()
    for copy in copies:
        copy.wait()
    if halo:
        for which in range(4):

            @pl.when(sends[which])
            def _(which=which):
                edge(which, col if which < 2 else row).wait_send()

            @pl.when(receives[which][0])
            def _(which=which):
                for slot in range(nx if which < 2 else ny):
                    edge(which, slot).wait_recv()


def exchange(xr, xc, call, edges=None):
    nx, ny = xr.shape[0], xc.shape[0]
    shapes = [xr.shape, xc.shape]
    sems = [(nx - 1,), (nx - 1,), (ny - 1,), (ny - 1,), (2,)]
    args = [xr, xc]
    if edges is not None:
        args += list(edges)
        shapes += [(2 * nx,) + edges[0].shape[1:], (2 * ny,) + edges[1].shape[1:]]
        sems += [(4,), (2 * nx,), (2 * ny,)]
    return pl.pallas_call(
        functools.partial(exchange_kernel, nx, ny, edges is not None),
        out_shape=tuple(jax.ShapeDtypeStruct(shape, xr.dtype) for shape in shapes),
        in_specs=[pl.BlockSpec(memory_space=pltpu.VMEM)] * len(args),
        out_specs=(pl.BlockSpec(memory_space=pltpu.VMEM),) * len(shapes),
        scratch_shapes=[pltpu.SemaphoreType.DMA(shape) for shape in sems],
        compiler_params=pltpu.CompilerParams(
            collective_id=call, has_side_effects=True, vmem_limit_bytes=16 * 2**20
        ),
    )(*args)


def scan_kernel(
    states, chunk, step_r, drive_r, coef_r, rate_r, step_c, drive_c, coef_c, rate_c, y_r, y_c, pick, wide, state_ref
):
    place = lax.broadcasted_iota(jnp.int32, pick.shape, 0)
    lane = lax.broadcasted_iota(jnp.int32, pick.shape, 1)
    pick[...] = jnp.where(lax.rem(place, 2 * states) == lane // LANES, 1.0, 0.0).astype(jnp.bfloat16)

    def run(step, drive, coef, rate, out):
        length, lines, lanes = step.shape
        copies = lanes // LANES
        state_ref[...] = jnp.zeros_like(state_ref)

        @pl.loop(0, length // chunk)
        def _(block):
            rows = chunk * lines
            values = coef[pl.ds(pl.multiple_of(block * rows, rows), rows), :]
            high = values.astype(jnp.bfloat16)
            rest = values - high.astype(jnp.float32)
            middle = rest.astype(jnp.bfloat16)
            low = (rest - middle.astype(jnp.float32)).astype(jnp.bfloat16)
            parts = jnp.concatenate([high, middle, low], axis=1)
            wide[...] = jnp.dot(parts, pick[...], preferred_element_type=jnp.float32)

            def advance(k, state):
                t = block * chunk + k
                at = pl.ds(pl.multiple_of(k * lines, lines), lines)
                size, push = step[t], drive[t]
                new, sums = [], [None, None]
                for n in range(states):
                    into = wide[at, n * LANES : (n + 1) * LANES]
                    outof = wide[at, (states + n) * LANES : (states + n + 1) * LANES]
                    if copies > 1:
                        into = jnp.concatenate([into] * copies, axis=1)
                        outof = jnp.concatenate([outof] * copies, axis=1)
                    now = jnp.exp2(size * rate[n]) * state[n] + push * into
                    new.append(now)
                    term = now * outof
                    sums[n % 2] = term if sums[n % 2] is None else sums[n % 2] + term
                out[t] = sums[0] + sums[1]
                return tuple(new)

            start = tuple(state_ref[n, :, :lanes] for n in range(states))
            end = lax.fori_loop(0, chunk, advance, start, unroll=4)
            for n in range(states):
                state_ref[n, :, :lanes] = end[n]

    run(step_r, drive_r, coef_r, rate_r, y_r)
    run(step_c, drive_c, coef_c, rate_c, y_c)


def scans(row_args, col_args, states):
    lines = row_args[0].shape[1]
    chunk = math.gcd(16, math.gcd(row_args[0].shape[0], col_args[0].shape[0]))
    return pl.pallas_call(
        functools.partial(scan_kernel, states, chunk),
        out_shape=(
            jax.ShapeDtypeStruct(row_args[0].shape, jnp.float32),
            jax.ShapeDtypeStruct(col_args[0].shape, jnp.float32),
        ),
        in_specs=[pl.BlockSpec(memory_space=pltpu.VMEM)] * 8,
        out_specs=(pl.BlockSpec(memory_space=pltpu.VMEM),) * 2,
        scratch_shapes=[
            pltpu.VMEM((6 * states, 2 * states * LANES), jnp.bfloat16),
            pltpu.VMEM((chunk * lines, 2 * states * LANES), jnp.float32),
            pltpu.VMEM((states, lines, max(row_args[0].shape[2], col_args[0].shape[2])), jnp.float32),
        ],
        compiler_params=pltpu.CompilerParams(vmem_limit_bytes=32 * 2**20),
    )(*row_args, *col_args)


def to_tile(values, axis):
    pads = [(0, 0)] * values.ndim
    pads[axis] = (0, -values.shape[axis] % 8)
    return jnp.pad(values, pads)


def fold(values, lanes):
    _, lines, length, channels = values.shape
    parts = channels // lanes
    flipped = jnp.stack([values[0], jnp.flip(values[1], 1)])
    split = flipped.reshape(2, lines, length, parts, lanes)
    return to_tile(split.transpose(2, 3, 0, 1, 4).reshape(length, parts * 2 * lines, lanes), 1)


def strip_inputs(feats, codes, conv, weights, first, lanes):
    (norm_gain, in_weight, conv_bias, proj_weight, step_weight, step_bias, code_table, decay_rates) = weights
    lines, length = codes.shape
    inner_width = in_weight.shape[1] // 2
    states, low_rank = decay_rates.shape[1], step_weight.shape[1]
    halves = inner_width // lanes
    wide = low_rank + 2 * states
    normed = layer_norm(feats.astype(jnp.float32), norm_gain).astype(jnp.bfloat16)
    inner = jnp.dot(
        normed.reshape(-1, feats.shape[2]),
        in_weight[:, :inner_width],
        preferred_element_type=jnp.float32,
    ).astype(jnp.bfloat16)
    inner = inner.reshape(lines + 2, length, inner_width)
    padded = jnp.pad(inner, ((0, 0), (1, 1), (0, 0)))
    summed = jnp.zeros((lines, length, inner_width), jnp.float32) + conv_bias
    for a in range(3):
        for b in range(3):
            summed = (
                summed + padded[a : a + lines, b : b + length].astype(jnp.float32) * conv[a, b]
            )
    signal_low = jax.nn.silu(summed).astype(jnp.bfloat16)
    signal = signal_low.astype(jnp.float32)
    coefs = jnp.dot(
        signal_low.reshape(-1, inner_width),
        proj_weight[:, first * wide : (first + 2) * wide],
        preferred_element_type=jnp.float32,
    ).reshape(lines, length, 2, wide)
    one_hot = (codes[:, :, None] == jnp.arange(code_table.shape[0])).astype(jnp.float32)
    offsets = jnp.einsum("pqk,ke->pqe", one_hot, code_table, precision=lax.Precision.HIGHEST)
    step = jax.nn.softplus(
        jnp.einsum(
            "pqdr,dre->dpqe",
            coefs[..., :low_rank],
            step_weight[first : first + 2],
            precision=lax.Precision.HIGHEST,
        )
        + step_bias[first : first + 2, None, None, :]
        + offsets
    )
    mix = coefs[..., low_rank:].transpose(2, 0, 1, 3)
    mix = jnp.stack([mix[0], jnp.flip(mix[1], 1)]).transpose(2, 0, 1, 3)
    mix = mix.reshape(length, 1, 2 * lines, 2 * states)
    mix = jnp.broadcast_to(mix, (length, halves, 2 * lines, 2 * states))
    mix = to_tile(mix.reshape(length, halves * 2 * lines, 2 * states), 1).reshape(-1, 2 * states)
    rate = (decay_rates[first : first + 2] * (-1.0 / math.log(2.0))).reshape(2, states, halves, lanes)
    rate = jnp.broadcast_to(
        rate.transpose(1, 2, 0, 3)[:, :, :, None, :], (states, halves, 2, lines, lanes)
    ).reshape(states, halves * 2 * lines, lanes)
    return (fold(step, lanes), fold(step * signal, lanes), mix, to_tile(rate, 1)), signal


def unfold(y, lines, channels):
    length, _, lanes = y.shape
    parts = channels // lanes
    y = y[:, : parts * 2 * lines].reshape(length, parts, 2, lines, lanes)
    y = y[:, :, 0] + jnp.flip(y[:, :, 1], 0)
    return y.transpose(2, 0, 1, 3).reshape(lines, length, channels)


def on_device(
    features,
    scene_codes,
    norm_gain,
    in_weight,
    conv_weight,
    conv_bias,
    proj_weight,
    step_weight,
    step_bias,
    code_table,
    decay_rates,
    skip_gain,
    out_gain,
    out_weight,
):
    nx, ny = lax.axis_size("gx"), lax.axis_size("gy")
    rows, cols, width = features.shape
    inner_width = in_weight.shape[1] // 2
    states = decay_rates.shape[1]
    rp, cp = rows // nx, cols // ny
    codes = scene_codes.astype(jnp.bfloat16)

    def payload(block, code):
        lines, length, _ = block.shape
        size = -(-(length + 1) // 16) * 16
        code = jnp.pad(code[:, None, :], ((0, 0), (0, size - length - 1), (0, width - length)))
        return jnp.concatenate([block, code], axis=1)

    row_load = payload(features, codes)
    col_load = payload(jnp.swapaxes(features, 0, 1), codes.T)
    row_size, col_size = row_load.shape[1], col_load.shape[1]
    edges = tuple(jnp.stack([load[0], load[-1]]) for load in (row_load, col_load))
    row_load, col_load = (jnp.pad(load, ((1, 1), (0, 0), (0, 0))) for load in (row_load, col_load))
    xr = jnp.stack([row_load[k * rp : k * rp + rp + 2] for k in range(nx)])
    xc = jnp.stack([col_load[k * cp : k * cp + cp + 2] for k in range(ny)])
    got_r, got_c, halo_r, halo_c = exchange(
        xr.reshape(nx, (rp + 2) * row_size, width),
        xc.reshape(ny, (cp + 2) * col_size, width),
        0,
        edges,
    )
    place_x, place_y = lax.axis_index("gx"), lax.axis_index("gy")

    def assembled(got, halo, parts, lines, size, length, inner, outer, inner_count, outer_count):
        got = got.reshape(parts, lines + 2, size, width)
        code = got[:, 1:-1, length, :length].transpose(1, 0, 2).reshape(lines, parts * length)
        feats = got[:, :, :length].transpose(1, 0, 2, 3)
        none = jnp.zeros_like(feats[0])
        halo = halo.reshape(2, parts, size, width)
        before = jnp.where(outer > 0, halo[0, :, :length], none)
        after = jnp.where(outer < outer_count - 1, halo[1, :, :length], none)
        feats = jnp.concatenate(
            [
                jnp.where(inner == 0, before, feats[0])[None],
                feats[1:-1],
                jnp.where(inner == inner_count - 1, after, feats[-1])[None],
            ]
        )
        return feats.reshape(lines + 2, parts * length, width), code.astype(jnp.int32)

    weights = (
        norm_gain, in_weight, conv_bias, proj_weight, step_weight, step_bias, code_table, decay_rates,
    )
    feats_r, codes_r = assembled(
        got_r, halo_r, nx, rp, row_size, cols, place_x, place_y, nx, ny
    )
    feats_c, codes_c = assembled(
        got_c, halo_c, ny, cp, col_size, rows, place_y, place_x, ny, nx
    )
    row_args, signal_r = strip_inputs(feats_r, codes_r, conv_weight, weights, 0, LANES)
    col_args, signal_c = strip_inputs(feats_c, codes_c, jnp.swapaxes(conv_weight, 0, 1), weights, 2, inner_width)
    y_r, y_c = scans(row_args, col_args, states)
    y_r = unfold(y_r, rp, inner_width) + (skip_gain[0] + skip_gain[1]) * signal_r
    y_c = unfold(y_c, cp, inner_width) + (skip_gain[2] + skip_gain[3]) * signal_c
    y_r = y_r.astype(jnp.bfloat16).reshape(rp, nx, cols, inner_width).transpose(1, 0, 2, 3)
    y_c = y_c.astype(jnp.bfloat16).reshape(cp, ny, rows, inner_width).transpose(1, 0, 2, 3)
    back_r, back_c = exchange(
        y_r.reshape(nx, rp * cols, inner_width), y_c.reshape(ny, cp * rows, inner_width), 1
    )
    back_r = back_r.astype(jnp.float32).reshape(rows, cols, inner_width)
    back_c = back_c.astype(jnp.float32).reshape(cols, rows, inner_width)
    total = back_r + jnp.swapaxes(back_c, 0, 1)

    source = features.astype(jnp.float32)
    normed = layer_norm(source, norm_gain).astype(jnp.bfloat16)
    gate = jnp.dot(
        normed.reshape(-1, width), in_weight[:, inner_width:], preferred_element_type=jnp.float32
    ).astype(jnp.bfloat16).reshape(rows, cols, inner_width)
    normed_out = layer_norm(total, out_gain)
    mixed = (normed_out * jax.nn.silu(gate.astype(jnp.float32))).astype(jnp.bfloat16)
    added = jnp.dot(
        mixed.reshape(-1, inner_width), out_weight, preferred_element_type=jnp.float32
    ).reshape(rows, cols, width)
    return (source + added).astype(jnp.bfloat16)


def solution(mesh):
    placed = (P(("groups", "gy"), "gx", None), P(("groups", "gy"), "gx")) + (P(),) * 12
    return jax.shard_map(
        on_device,
        mesh=mesh,
        in_specs=placed,
        out_specs=P(("groups", "gy"), "gx", None),
        check_vma=False,
    )
```

```python
import functools
import math

import jax
import jax.numpy as jnp
from jax import lax
from jax.experimental import pallas as pl
from jax.experimental.pallas import tpu as pltpu
from jax.sharding import PartitionSpec as P

MESH = pl.DeviceIdType.MESH
LANES = 128


def layer_norm(values, gain):
    mean = jnp.mean(values, axis=-1, keepdims=True)
    centered = values - mean
    spread = jnp.mean(centered * centered, axis=-1, keepdims=True)
    return centered * lax.rsqrt(spread + 1e-05) * gain


def exchange_kernel(nx, ny, halo, *refs):
    refs = list(refs)
    take = lambda count: [refs.pop(0) for _ in range(count)]
    xr, xc = take(2)
    edge_r, edge_c = take(2) if halo else (None, None)
    out_r, out_c = take(2)
    halo_r, halo_c = take(2) if halo else (None, None)
    send_r, recv_r, send_c, recv_c, own_sem = take(5)
    edge_sem, halo_r_sem, halo_c_sem = take(3) if halo else (None,) * 3
    group = lax.axis_index("groups")
    row = lax.axis_index("gy")
    col = lax.axis_index("gx")
    barrier = pltpu.get_barrier_semaphore()
    inside_up, inside_down = row > 0, row < ny - 1
    inside_left, inside_right = col > 0, col < nx - 1

    def greet(to_row, to_col):
        pl.semaphore_signal(barrier, inc=1, device_id=(group, to_row, to_col), device_id_type=MESH)

    for k in range(1, nx):
        greet(row, lax.rem(col + k, nx))
    for k in range(1, ny):
        greet(lax.rem(row + k, ny), col)
    if halo:
        receives = (
            (inside_up & (col == 0), [(lax.rem(row + ny - 1, ny), s) for s in range(nx)]),
            (inside_down & (col == nx - 1), [(lax.rem(row + 1, ny), s) for s in range(nx)]),
            (inside_left & (row == 0), [(s, lax.rem(col + nx - 1, nx)) for s in range(ny)]),
            (inside_right & (row == ny - 1), [(s, lax.rem(col + 1, nx)) for s in range(ny)]),
        )
        for here, sources in receives:

            @pl.when(here)
            def _(sources=sources):
                for source in sources:
                    greet(*source)

    own_r = pltpu.make_async_copy(xr.at[col], out_r.at[col], own_sem.at[0])
    own_c = pltpu.make_async_copy(xc.at[row], out_c.at[row], own_sem.at[1])
    own_r.start()
    own_c.start()
    peers = nx + ny - 2
    if halo:
        peers += lax.div(row + ny - 1, ny) + 1 - lax.div(row + 1, ny)
        peers += lax.div(col + nx - 1, nx) + 1 - lax.div(col + 1, nx)
    pl.semaphore_wait(barrier, peers)
    copies = []
    if halo:
        def edge(which, slot):
            down = which % 2 == 0
            if which < 2:
                return pltpu.make_async_remote_copy(
                    src_ref=edge_r.at[1 if down else 0],
                    dst_ref=halo_r.at[which * nx + slot],
                    send_sem=edge_sem.at[which],
                    recv_sem=halo_r_sem.at[which * nx + slot],
                    device_id=(group, lax.rem(row + (1 if down else ny - 1), ny), 0 if down else nx - 1),
                    device_id_type=MESH,
                )
            return pltpu.make_async_remote_copy(
                src_ref=edge_c.at[1 if down else 0],
                dst_ref=halo_c.at[(which - 2) * ny + slot],
                send_sem=edge_sem.at[which],
                recv_sem=halo_c_sem.at[(which - 2) * ny + slot],
                device_id=(group, 0 if down else ny - 1, lax.rem(col + (1 if down else nx - 1), nx)),
                device_id_type=MESH,
            )

        sends = (inside_down, inside_up, inside_right, inside_left)
        for which in range(4):

            @pl.when(sends[which])
            def _(which=which):
                edge(which, col if which < 2 else row).start()

    for k in range(1, ny):
        to = lax.rem(row + k, ny)
        copies.append(
            pltpu.make_async_remote_copy(
                src_ref=xc.at[to],
                dst_ref=out_c.at[row],
                send_sem=send_c.at[k - 1],
                recv_sem=recv_c.at[k - 1],
                device_id=(group, to, col),
                device_id_type=MESH,
            )
        )
        copies[-1].start()
    for k in range(1, nx):
        to = lax.rem(col + k, nx)
        copies.append(
            pltpu.make_async_remote_copy(
                src_ref=xr.at[to],
                dst_ref=out_r.at[col],
                send_sem=send_r.at[k - 1],
                recv_sem=recv_r.at[k - 1],
                device_id=(group, row, to),
                device_id_type=MESH,
            )
        )
        copies[-1].start()
    own_r.wait()
    own_c.wait()
    for copy in copies:
        copy.wait()
    if halo:
        for which in range(4):

            @pl.when(sends[which])
            def _(which=which):
                edge(which, col if which < 2 else row).wait_send()

            @pl.when(receives[which][0])
            def _(which=which):
                for slot in range(nx if which < 2 else ny):
                    edge(which, slot).wait_recv()


def exchange(xr, xc, call, edges=None):
    nx, ny = xr.shape[0], xc.shape[0]
    shapes = [xr.shape, xc.shape]
    sems = [(nx - 1,), (nx - 1,), (ny - 1,), (ny - 1,), (2,)]
    args = [xr, xc]
    if edges is not None:
        args += list(edges)
        shapes += [(2 * nx,) + edges[0].shape[1:], (2 * ny,) + edges[1].shape[1:]]
        sems += [(4,), (2 * nx,), (2 * ny,)]
    return pl.pallas_call(
        functools.partial(exchange_kernel, nx, ny, edges is not None),
        out_shape=tuple(jax.ShapeDtypeStruct(shape, xr.dtype) for shape in shapes),
        in_specs=[pl.BlockSpec(memory_space=pltpu.VMEM)] * len(args),
        out_specs=(pl.BlockSpec(memory_space=pltpu.VMEM),) * len(shapes),
        scratch_shapes=[pltpu.SemaphoreType.DMA(shape) for shape in sems],
        compiler_params=pltpu.CompilerParams(
            collective_id=call, has_side_effects=True, vmem_limit_bytes=16 * 2**20
        ),
    )(*args)


def to_eight(count):
    return -(-count // 8) * 8


def strip_kernel(
    states, low_rank, chunk,
    feats_r, codes_r, feats_c, codes_c,
    norm_gain, in_weight, conv_weight, conv_bias, proj, step_weight, step_bias, code_table,
    decay_rates, skip_gain,
    y_r, y_c,
    pick, wide, state_ref, inner_r, inner_c, sig_r, sig_c, step_r, step_c, drive_r, drive_c,
    coef_r, coef_c, rate_r, rate_c, out_r, out_c,
):
    place = lax.broadcasted_iota(jnp.int32, pick.shape, 0)
    lane = lax.broadcasted_iota(jnp.int32, pick.shape, 1)
    pick[...] = jnp.where(lax.rem(place, 2 * states) == lane // LANES, 1.0, 0.0).astype(jnp.bfloat16)
    inner_width = code_table.shape[1]
    halves = inner_width // LANES
    exact = lax.Precision.HIGHEST

    def run(feats, codes, inner_ref, sig, step, drive, coef, rate, out, y, first):
        lines, length = feats.shape[0] - 2, feats.shape[1]
        copies = step.shape[0]
        inside = halves // copies
        used = inside * 2 * lines
        rows = step.shape[1] // length
        if used < rows:
            for ref in (step, drive, coef, rate):
                ref[...] = jnp.zeros_like(ref)
        inner_ref[:, :8, :] = jnp.zeros((lines + 2, 8, inner_width), jnp.float32)
        inner_ref[:, 8 + length :, :] = jnp.zeros((lines + 2, 8, inner_width), jnp.float32)
        for line in range(lines + 2):
            normed = layer_norm(feats[line].astype(jnp.float32), norm_gain[...])
            inner = jnp.dot(
                normed.astype(jnp.bfloat16),
                in_weight[:, :inner_width],
                preferred_element_type=jnp.float32,
            )
            inner_ref[line, 8 : 8 + length, :] = inner.astype(jnp.bfloat16).astype(jnp.float32)
        at_row = lax.broadcasted_iota(jnp.int32, (length, length), 0)
        at_col = lax.broadcasted_iota(jnp.int32, (length, length), 1)
        turn = jnp.where(at_row + at_col == length - 1, 1.0, 0.0)

        def slots(line, d, half):
            part, inner_half = half % copies, half // copies
            return part, (inner_half * 2 + d) * lines + line

        for d in range(2):
            for half in range(halves):
                for line in range(lines):
                    part, slot = slots(line, d, half)
                    rate[part, pl.ds(slot, states, stride=rows), :] = decay_rates[
                        first + d, :, half * LANES : (half + 1) * LANES
                    ] * (-1.0 / math.log(2.0))
        for line in range(lines):
            summed = jnp.zeros((length, inner_width), jnp.float32) + conv_bias[...]
            for i in range(3):
                for j in range(3):
                    tap = i * 3 + j if first == 0 else j * 3 + i
                    summed = summed + (
                        inner_ref[line + i, 7 + j : 7 + j + length, :] * conv_weight[tap : tap + 1, :]
                    )
            signal_low = jax.nn.silu(summed).astype(jnp.bfloat16)
            signal = signal_low.astype(jnp.float32)
            sig[line] = signal
            hot = codes[line * length : (line + 1) * length, :] == lax.broadcasted_iota(
                jnp.int32, (length, code_table.shape[0]), 1
            )
            offsets = jnp.dot(
                jnp.where(hot, 1.0, 0.0), code_table[...],
                precision=exact, preferred_element_type=jnp.float32,
            )
            for d in range(2):
                way = first + d
                mix = jnp.dot(
                    signal_low,
                    proj[:, way * LANES : (way + 1) * LANES],
                    preferred_element_type=jnp.float32,
                )
                raw = (
                    jnp.dot(
                        mix[:, 2 * states : 2 * states + low_rank],
                        step_weight[way],
                        precision=exact,
                        preferred_element_type=jnp.float32,
                    )
                    + step_bias[way : way + 1, :]
                    + offsets
                )
                size = jnp.maximum(raw, 0.0) + jnp.log1p(jnp.exp(-jnp.abs(raw)))
                push = size * signal
                if d == 1:
                    size, push, mix = (
                        jnp.dot(turn, v, precision=exact, preferred_element_type=jnp.float32)
                        for v in (size, push, mix)
                    )
                for half in range(halves):
                    part, slot = slots(line, d, half)
                    at = pl.ds(slot, length, stride=rows)
                    step[part, at, :] = size[:, half * LANES : (half + 1) * LANES]
                    drive[part, at, :] = push[:, half * LANES : (half + 1) * LANES]
                    if part == 0:
                        coef[at, :] = mix

        state_ref[...] = jnp.zeros_like(state_ref)

        @pl.loop(0, length // chunk)
        def _(block):
            span = chunk * rows
            values = coef[pl.ds(pl.multiple_of(block * span, span), span), :][:, : 2 * states]
            high = values.astype(jnp.bfloat16)
            rest = values - high.astype(jnp.float32)
            middle = rest.astype(jnp.bfloat16)
            low = (rest - middle.astype(jnp.float32)).astype(jnp.bfloat16)
            parts = jnp.concatenate([high, middle, low], axis=1)
            wide[:span, :] = jnp.dot(parts, pick[...], preferred_element_type=jnp.float32)

            def advance(k, state):
                at = pl.ds(pl.multiple_of(k * rows, rows), rows)
                now_at = pl.ds(pl.multiple_of((block * chunk + k) * rows, rows), rows)
                size = [step[p, now_at, :] for p in range(copies)]
                push = [drive[p, now_at, :] for p in range(copies)]
                new = []
                sums = [[None, None] for _ in range(copies)]
                for n in range(states):
                    into = wide[at, n * LANES : (n + 1) * LANES]
                    outof = wide[at, (states + n) * LANES : (states + n + 1) * LANES]
                    for p in range(copies):
                        decay = jnp.exp2(size[p] * rate[p, n * rows : (n + 1) * rows, :])
                        now = decay * state[n * copies + p] + push[p] * into
                        new.append(now)
                        term = now * outof
                        old = sums[p][n % 2]
                        sums[p][n % 2] = term if old is None else old + term
                for p in range(copies):
                    out[p, now_at, :] = sums[p][0] + sums[p][1]
                return tuple(new)

            start = tuple(state_ref[k, :rows, :] for k in range(states * copies))
            end = lax.fori_loop(0, chunk, advance, start, unroll=4)
            for k in range(states * copies):
                state_ref[k, :rows, :] = end[k]

        direct = skip_gain[first : first + 1, :] + skip_gain[first + 1 : first + 2, :]
        for line in range(lines):
            for half in range(halves):
                lanes = slice(half * LANES, (half + 1) * LANES)
                part, slot = slots(line, 0, half)
                forward = out[part, pl.ds(slot, length, stride=rows), :]
                part, slot = slots(line, 1, half)
                back = jnp.dot(
                    turn,
                    out[part, pl.ds(slot, length, stride=rows), :],
                    precision=exact,
                    preferred_element_type=jnp.float32,
                )
                total = forward + back + direct[:, lanes] * sig[line, :, lanes]
                y[line, :, lanes] = total.astype(jnp.bfloat16)

    run(feats_r, codes_r, inner_r, sig_r, step_r, drive_r, coef_r, rate_r, out_r, y_r, 0)
    run(feats_c, codes_c, inner_c, sig_c, step_c, drive_c, coef_c, rate_c, out_c, y_c, 2)


def strips(feats_r, codes_r, feats_c, codes_c, weights, states, low_rank):
    inner_width = weights[1].shape[1] // 2
    halves = inner_width // LANES
    lengths = [feats_r.shape[1], feats_c.shape[1]]
    lines = [feats_r.shape[0] - 2, feats_c.shape[0] - 2]
    copies = [1, halves]
    rows = [to_eight(halves // c * 2 * n) for c, n in zip(copies, lines)]
    chunk = math.gcd(16, math.gcd(*lengths))

    def pair(shape):
        return [pltpu.VMEM(shape(lines[k], lengths[k], copies[k], rows[k]), jnp.float32) for k in (0, 1)]

    args = (feats_r, codes_r, feats_c, codes_c) + weights
    return pl.pallas_call(
        functools.partial(strip_kernel, states, low_rank, chunk),
        out_shape=tuple(
            jax.ShapeDtypeStruct((lines[k], lengths[k], inner_width), jnp.bfloat16) for k in (0, 1)
        ),
        in_specs=[pl.BlockSpec(memory_space=pltpu.VMEM)] * len(args),
        out_specs=(pl.BlockSpec(memory_space=pltpu.VMEM),) * 2,
        scratch_shapes=[
            pltpu.VMEM((6 * states, 2 * states * LANES), jnp.bfloat16),
            pltpu.VMEM((chunk * max(rows), 2 * states * LANES), jnp.float32),
            pltpu.VMEM((states * halves, max(rows), LANES), jnp.float32),
            *pair(lambda n, t, c, r: (n + 2, t + 16, inner_width)),
            *pair(lambda n, t, c, r: (n, t, inner_width)),
            *pair(lambda n, t, c, r: (c, t * r, LANES)),
            *pair(lambda n, t, c, r: (c, t * r, LANES)),
            *pair(lambda n, t, c, r: (t * r, LANES)),
            *pair(lambda n, t, c, r: (c, states * r, LANES)),
            *pair(lambda n, t, c, r: (c, t * r, LANES)),
        ],
        compiler_params=pltpu.CompilerParams(vmem_limit_bytes=40 * 2**20),
    )(*args)


def on_device(
    features,
    scene_codes,
    norm_gain,
    in_weight,
    conv_weight,
    conv_bias,
    proj_weight,
    step_weight,
    step_bias,
    code_table,
    decay_rates,
    skip_gain,
    out_gain,
    out_weight,
):
    nx, ny = lax.axis_size("gx"), lax.axis_size("gy")
    rows, cols, width = features.shape
    inner_width = in_weight.shape[1] // 2
    states = decay_rates.shape[1]
    rp, cp = rows // nx, cols // ny
    codes = scene_codes.astype(jnp.bfloat16)

    def payload(block, code):
        lines, length, _ = block.shape
        size = -(-(length + 1) // 16) * 16
        code = jnp.pad(code[:, None, :], ((0, 0), (0, size - length - 1), (0, width - length)))
        return jnp.concatenate([block, code], axis=1)

    row_load = payload(features, codes)
    col_load = payload(jnp.swapaxes(features, 0, 1), codes.T)
    row_size, col_size = row_load.shape[1], col_load.shape[1]
    edges = tuple(jnp.stack([load[0], load[-1]]) for load in (row_load, col_load))
    row_load, col_load = (jnp.pad(load, ((1, 1), (0, 0), (0, 0))) for load in (row_load, col_load))
    xr = jnp.stack([row_load[k * rp : k * rp + rp + 2] for k in range(nx)])
    xc = jnp.stack([col_load[k * cp : k * cp + cp + 2] for k in range(ny)])
    got_r, got_c, halo_r, halo_c = exchange(
        xr.reshape(nx, (rp + 2) * row_size, width),
        xc.reshape(ny, (cp + 2) * col_size, width),
        0,
        edges,
    )
    place_x, place_y = lax.axis_index("gx"), lax.axis_index("gy")

    def assembled(got, halo, parts, lines, size, length, inner, outer, inner_count, outer_count):
        got = got.reshape(parts, lines + 2, size, width)
        code = got[:, 1:-1, length, :length].transpose(1, 0, 2).reshape(lines, parts * length)
        feats = got[:, :, :length].transpose(1, 0, 2, 3)
        none = jnp.zeros_like(feats[0])
        halo = halo.reshape(2, parts, size, width)
        before = jnp.where(outer > 0, halo[0, :, :length], none)
        after = jnp.where(outer < outer_count - 1, halo[1, :, :length], none)
        feats = jnp.concatenate(
            [
                jnp.where(inner == 0, before, feats[0])[None],
                feats[1:-1],
                jnp.where(inner == inner_count - 1, after, feats[-1])[None],
            ]
        )
        return feats.reshape(lines + 2, parts * length, width), code.astype(jnp.int32)

    low_rank = step_weight.shape[1]
    proj = proj_weight.reshape(inner_width, -1, low_rank + 2 * states)
    proj = jnp.concatenate([proj[..., low_rank:], proj[..., :low_rank]], axis=-1)
    proj = jnp.pad(proj, ((0, 0), (0, 0), (0, LANES - low_rank - 2 * states)))
    weights = (
        norm_gain[None, :], in_weight, conv_weight.reshape(9, inner_width), conv_bias[None, :],
        proj.reshape(inner_width, -1), step_weight, step_bias, code_table, decay_rates, skip_gain,
    )
    feats_r, codes_r = assembled(
        got_r, halo_r, nx, rp, row_size, cols, place_x, place_y, nx, ny
    )
    feats_c, codes_c = assembled(
        got_c, halo_c, ny, cp, col_size, rows, place_y, place_x, ny, nx
    )
    y_r, y_c = strips(
        feats_r, codes_r.reshape(-1, 1), feats_c, codes_c.reshape(-1, 1), weights, states, low_rank
    )
    y_r = y_r.reshape(rp, nx, cols, inner_width).transpose(1, 0, 2, 3)
    y_c = y_c.reshape(cp, ny, rows, inner_width).transpose(1, 0, 2, 3)
    back_r, back_c = exchange(
        y_r.reshape(nx, rp * cols, inner_width), y_c.reshape(ny, cp * rows, inner_width), 1
    )
    back_r = back_r.astype(jnp.float32).reshape(rows, cols, inner_width)
    back_c = back_c.astype(jnp.float32).reshape(cols, rows, inner_width)
    total = back_r + jnp.swapaxes(back_c, 0, 1)

    source = features.astype(jnp.float32)
    normed = layer_norm(source, norm_gain).astype(jnp.bfloat16)
    gate = jnp.dot(
        normed.reshape(-1, width), in_weight[:, inner_width:], preferred_element_type=jnp.float32
    ).astype(jnp.bfloat16).reshape(rows, cols, inner_width)
    normed_out = layer_norm(total, out_gain)
    mixed = (normed_out * jax.nn.silu(gate.astype(jnp.float32))).astype(jnp.bfloat16)
    added = jnp.dot(
        mixed.reshape(-1, inner_width), out_weight, preferred_element_type=jnp.float32
    ).reshape(rows, cols, width)
    return (source + added).astype(jnp.bfloat16)


def solution(mesh):
    placed = (P(("groups", "gy"), "gx", None), P(("groups", "gy"), "gx")) + (P(),) * 12
    return jax.shard_map(
        on_device,
        mesh=mesh,
        in_specs=placed,
        out_specs=P(("groups", "gy"), "gx", None),
        check_vma=False,
    )
```

```python
import functools
import math

import jax
import jax.numpy as jnp
from jax import lax
from jax.experimental import pallas as pl
from jax.experimental.pallas import tpu as pltpu
from jax.sharding import PartitionSpec as P

MESH = pl.DeviceIdType.MESH
LANES = 128


def layer_norm(values, gain):
    mean = jnp.mean(values, axis=-1, keepdims=True)
    centered = values - mean
    spread = jnp.mean(centered * centered, axis=-1, keepdims=True)
    return centered * lax.rsqrt(spread + 1e-05) * gain


def exchange_kernel(nx, ny, halo, *refs):
    refs = list(refs)
    take = lambda count: [refs.pop(0) for _ in range(count)]
    xr, xc = take(2)
    edge_r, edge_c = take(2) if halo else (None, None)
    out_r, out_c = take(2)
    halo_r, halo_c = take(2) if halo else (None, None)
    send_r, recv_r, send_c, recv_c, own_sem = take(5)
    edge_sem, halo_r_sem, halo_c_sem = take(3) if halo else (None,) * 3
    group = lax.axis_index("groups")
    row = lax.axis_index("gy")
    col = lax.axis_index("gx")
    barrier = pltpu.get_barrier_semaphore()
    inside_up, inside_down = row > 0, row < ny - 1
    inside_left, inside_right = col > 0, col < nx - 1

    def greet(to_row, to_col):
        pl.semaphore_signal(barrier, inc=1, device_id=(group, to_row, to_col), device_id_type=MESH)

    for k in range(1, nx):
        greet(row, lax.rem(col + k, nx))
    for k in range(1, ny):
        greet(lax.rem(row + k, ny), col)
    if halo:
        receives = (
            (inside_up & (col == 0), [(lax.rem(row + ny - 1, ny), s) for s in range(nx)]),
            (inside_down & (col == nx - 1), [(lax.rem(row + 1, ny), s) for s in range(nx)]),
            (inside_left & (row == 0), [(s, lax.rem(col + nx - 1, nx)) for s in range(ny)]),
            (inside_right & (row == ny - 1), [(s, lax.rem(col + 1, nx)) for s in range(ny)]),
        )
        for here, sources in receives:

            @pl.when(here)
            def _(sources=sources):
                for source in sources:
                    greet(*source)

    own_r = pltpu.make_async_copy(xr.at[col], out_r.at[col], own_sem.at[0])
    own_c = pltpu.make_async_copy(xc.at[row], out_c.at[row], own_sem.at[1])
    own_r.start()
    own_c.start()
    peers = nx + ny - 2
    if halo:
        peers += lax.div(row + ny - 1, ny) + 1 - lax.div(row + 1, ny)
        peers += lax.div(col + nx - 1, nx) + 1 - lax.div(col + 1, nx)
    pl.semaphore_wait(barrier, peers)
    copies = []
    if halo:
        def edge(which, slot):
            down = which % 2 == 0
            if which < 2:
                return pltpu.make_async_remote_copy(
                    src_ref=edge_r.at[1 if down else 0],
                    dst_ref=halo_r.at[which * nx + slot],
                    send_sem=edge_sem.at[which],
                    recv_sem=halo_r_sem.at[which * nx + slot],
                    device_id=(group, lax.rem(row + (1 if down else ny - 1), ny), 0 if down else nx - 1),
                    device_id_type=MESH,
                )
            return pltpu.make_async_remote_copy(
                src_ref=edge_c.at[1 if down else 0],
                dst_ref=halo_c.at[(which - 2) * ny + slot],
                send_sem=edge_sem.at[which],
                recv_sem=halo_c_sem.at[(which - 2) * ny + slot],
                device_id=(group, 0 if down else ny - 1, lax.rem(col + (1 if down else nx - 1), nx)),
                device_id_type=MESH,
            )

        sends = (inside_down, inside_up, inside_right, inside_left)
        for which in range(4):

            @pl.when(sends[which])
            def _(which=which):
                edge(which, col if which < 2 else row).start()

    for k in range(1, ny):
        to = lax.rem(row + k, ny)
        copies.append(
            pltpu.make_async_remote_copy(
                src_ref=xc.at[to],
                dst_ref=out_c.at[row],
                send_sem=send_c.at[k - 1],
                recv_sem=recv_c.at[k - 1],
                device_id=(group, to, col),
                device_id_type=MESH,
            )
        )
        copies[-1].start()
    for k in range(1, nx):
        to = lax.rem(col + k, nx)
        copies.append(
            pltpu.make_async_remote_copy(
                src_ref=xr.at[to],
                dst_ref=out_r.at[col],
                send_sem=send_r.at[k - 1],
                recv_sem=recv_r.at[k - 1],
                device_id=(group, row, to),
                device_id_type=MESH,
            )
        )
        copies[-1].start()
    own_r.wait()
    own_c.wait()
    for copy in copies:
        copy.wait()
    if halo:
        for which in range(4):

            @pl.when(sends[which])
            def _(which=which):
                edge(which, col if which < 2 else row).wait_send()

            @pl.when(receives[which][0])
            def _(which=which):
                for slot in range(nx if which < 2 else ny):
                    edge(which, slot).wait_recv()


def exchange(xr, xc, call, edges=None):
    nx, ny = xr.shape[0], xc.shape[0]
    shapes = [xr.shape, xc.shape]
    sems = [(nx - 1,), (nx - 1,), (ny - 1,), (ny - 1,), (2,)]
    args = [xr, xc]
    if edges is not None:
        args += list(edges)
        shapes += [(2 * nx,) + edges[0].shape[1:], (2 * ny,) + edges[1].shape[1:]]
        sems += [(4,), (2 * nx,), (2 * ny,)]
    return pl.pallas_call(
        functools.partial(exchange_kernel, nx, ny, edges is not None),
        out_shape=tuple(jax.ShapeDtypeStruct(shape, xr.dtype) for shape in shapes),
        in_specs=[pl.BlockSpec(memory_space=pltpu.VMEM)] * len(args),
        out_specs=(pl.BlockSpec(memory_space=pltpu.VMEM),) * len(shapes),
        scratch_shapes=[pltpu.SemaphoreType.DMA(shape) for shape in sems],
        compiler_params=pltpu.CompilerParams(
            collective_id=call, has_side_effects=True, vmem_limit_bytes=16 * 2**20
        ),
    )(*args)


def to_eight(count):
    return -(-count // 8) * 8


def chosen(picks, values):
    high = values.astype(jnp.bfloat16)
    rest = values - high.astype(jnp.float32)
    middle = rest.astype(jnp.bfloat16)
    low = (rest - middle.astype(jnp.float32)).astype(jnp.bfloat16)
    out = [jnp.dot(picks, part, preferred_element_type=jnp.float32) for part in (low, middle, high)]
    return (out[0] + out[1]) + out[2]


def strip_kernel(
    states, low_rank, chunk,
    feats_r, codes_r, feats_c, codes_c,
    norm_gain, in_weight, conv_weight, conv_bias, proj, step_weight, step_bias, code_table,
    decay_rates, skip_gain,
    y_r, y_c,
    pick, wide, state_ref, inner_r, inner_c, sig_r, sig_c, step_r, step_c, drive_r, drive_c,
    coef_r, coef_c, rate_r, rate_c, out_r, out_c,
):
    place = lax.broadcasted_iota(jnp.int32, pick.shape, 0)
    lane = lax.broadcasted_iota(jnp.int32, pick.shape, 1)
    pick[...] = jnp.where(lax.rem(place, 2 * states) == lane // LANES, 1.0, 0.0).astype(jnp.bfloat16)
    inner_width = code_table.shape[1]
    halves = inner_width // LANES
    exact = lax.Precision.HIGHEST

    def run(feats, codes, inner_ref, sig, step, drive, coef, rate, out, y, first):
        lines, length = feats.shape[0] - 2, feats.shape[1]
        copies = step.shape[0]
        inside = halves // copies
        used = inside * 2 * lines
        rows = step.shape[1] // length
        if used < rows:
            for ref in (step, drive, coef, rate):
                ref[...] = jnp.zeros_like(ref)
        inner_ref[:, :8, :] = jnp.zeros((lines + 2, 8, inner_width), jnp.float32)
        inner_ref[:, 8 + length :, :] = jnp.zeros((lines + 2, 8, inner_width), jnp.float32)
        for line in range(lines + 2):
            normed = layer_norm(feats[line].astype(jnp.float32), norm_gain[...])
            inner = jnp.dot(
                normed.astype(jnp.bfloat16),
                in_weight[:, :inner_width],
                preferred_element_type=jnp.float32,
            )
            inner_ref[line, 8 : 8 + length, :] = inner.astype(jnp.bfloat16).astype(jnp.float32)
        at_row = lax.broadcasted_iota(jnp.int32, (length, length), 0)
        at_col = lax.broadcasted_iota(jnp.int32, (length, length), 1)
        turn = jnp.where(at_row + at_col == length - 1, 1.0, 0.0).astype(jnp.bfloat16)
        hot = codes[...] == lax.broadcasted_iota(
            jnp.int32, (lines * length, code_table.shape[0]), 1
        )
        all_offsets = chosen(jnp.where(hot, 1.0, 0.0).astype(jnp.bfloat16), code_table[...])
        slot_at = lax.broadcasted_iota(jnp.int32, (rows, LANES), 0)
        ahead = lax.rem(slot_at // lines, 2) == 0

        def slots(line, d, half):
            part, inner_half = half % copies, half // copies
            return part, (inner_half * 2 + d) * lines + line

        for d in range(2):
            for half in range(halves):
                for line in range(lines):
                    part, slot = slots(line, d, half)
                    rate[part, pl.ds(slot, states, stride=rows), :] = decay_rates[
                        first + d, :, half * LANES : (half + 1) * LANES
                    ] * (-1.0 / math.log(2.0))
        for line in range(lines):
            summed = jnp.zeros((length, inner_width), jnp.float32) + conv_bias[...]
            for i in range(3):
                for j in range(3):
                    tap = i * 3 + j if first == 0 else j * 3 + i
                    summed = summed + (
                        inner_ref[line + i, 7 + j : 7 + j + length, :] * conv_weight[tap : tap + 1, :]
                    )
            signal_low = jax.nn.silu(summed).astype(jnp.bfloat16)
            signal = signal_low.astype(jnp.float32)
            sig[line] = signal
            offsets = all_offsets[line * length : (line + 1) * length, :]
            for d in range(2):
                way = first + d
                mix = jnp.dot(
                    signal_low,
                    proj[:, way * LANES : (way + 1) * LANES],
                    preferred_element_type=jnp.float32,
                )
                raw = (
                    jnp.dot(
                        mix[:, 2 * states : 2 * states + low_rank],
                        step_weight[way],
                        precision=exact,
                        preferred_element_type=jnp.float32,
                    )
                    + step_bias[way : way + 1, :]
                    + offsets
                )
                size = jnp.maximum(raw, 0.0) + jnp.log1p(jnp.exp(-jnp.abs(raw)))
                push = size * signal
                if d == 1:
                    mix = chosen(turn, mix)
                for half in range(halves):
                    part, slot = slots(line, d, half)
                    at = pl.ds(slot, length, stride=rows)
                    step[part, at, :] = size[:, half * LANES : (half + 1) * LANES]
                    drive[part, at, :] = push[:, half * LANES : (half + 1) * LANES]
                    if part == 0:
                        coef[at, :] = mix

        state_ref[...] = jnp.zeros_like(state_ref)

        @pl.loop(0, length // chunk)
        def _(block):
            span = chunk * rows
            values = coef[pl.ds(pl.multiple_of(block * span, span), span), :][:, : 2 * states]
            high = values.astype(jnp.bfloat16)
            rest = values - high.astype(jnp.float32)
            middle = rest.astype(jnp.bfloat16)
            low = (rest - middle.astype(jnp.float32)).astype(jnp.bfloat16)
            parts = jnp.concatenate([high, middle, low], axis=1)
            wide[:span, :] = jnp.dot(parts, pick[...], preferred_element_type=jnp.float32)

            def advance(k, state):
                at = pl.ds(pl.multiple_of(k * rows, rows), rows)
                now_at = pl.ds(pl.multiple_of((block * chunk + k) * rows, rows), rows)
                last_at = pl.ds(
                    pl.multiple_of((length - 1 - block * chunk - k) * rows, rows), rows
                )
                size, push = (
                    [jnp.where(ahead, ref[p, now_at, :], ref[p, last_at, :]) for p in range(copies)]
                    for ref in (step, drive)
                )
                new = []
                sums = [[None, None] for _ in range(copies)]
                for n in range(states):
                    into = wide[at, n * LANES : (n + 1) * LANES]
                    outof = wide[at, (states + n) * LANES : (states + n + 1) * LANES]
                    for p in range(copies):
                        decay = jnp.exp2(size[p] * rate[p, n * rows : (n + 1) * rows, :])
                        now = decay * state[n * copies + p] + push[p] * into
                        new.append(now)
                        term = now * outof
                        old = sums[p][n % 2]
                        sums[p][n % 2] = term if old is None else old + term
                for p in range(copies):
                    out[p, now_at, :] = sums[p][0] + sums[p][1]
                    out[copies + p, last_at, :] = sums[p][0] + sums[p][1]
                return tuple(new)

            start = tuple(state_ref[k, :rows, :] for k in range(states * copies))
            end = lax.fori_loop(0, chunk, advance, start, unroll=4)
            for k in range(states * copies):
                state_ref[k, :rows, :] = end[k]

        direct = skip_gain[first : first + 1, :] + skip_gain[first + 1 : first + 2, :]
        for line in range(lines):
            for half in range(halves):
                lanes = slice(half * LANES, (half + 1) * LANES)
                part, slot = slots(line, 0, half)
                forward = out[part, pl.ds(slot, length, stride=rows), :]
                part, slot = slots(line, 1, half)
                back = out[copies + part, pl.ds(slot, length, stride=rows), :]
                total = forward + back + direct[:, lanes] * sig[line, :, lanes]
                y[line, :, lanes] = total.astype(jnp.bfloat16)

    run(feats_r, codes_r, inner_r, sig_r, step_r, drive_r, coef_r, rate_r, out_r, y_r, 0)
    run(feats_c, codes_c, inner_c, sig_c, step_c, drive_c, coef_c, rate_c, out_c, y_c, 2)


def strips(feats_r, codes_r, feats_c, codes_c, weights, states, low_rank):
    inner_width = weights[1].shape[1] // 2
    halves = inner_width // LANES
    lengths = [feats_r.shape[1], feats_c.shape[1]]
    lines = [feats_r.shape[0] - 2, feats_c.shape[0] - 2]
    copies = [1, halves]
    rows = [to_eight(halves // c * 2 * n) for c, n in zip(copies, lines)]
    chunk = math.gcd(16, math.gcd(*lengths))

    def pair(shape):
        return [pltpu.VMEM(shape(lines[k], lengths[k], copies[k], rows[k]), jnp.float32) for k in (0, 1)]

    args = (feats_r, codes_r, feats_c, codes_c) + weights
    return pl.pallas_call(
        functools.partial(strip_kernel, states, low_rank, chunk),
        out_shape=tuple(
            jax.ShapeDtypeStruct((lines[k], lengths[k], inner_width), jnp.bfloat16) for k in (0, 1)
        ),
        in_specs=[pl.BlockSpec(memory_space=pltpu.VMEM)] * len(args),
        out_specs=(pl.BlockSpec(memory_space=pltpu.VMEM),) * 2,
        scratch_shapes=[
            pltpu.VMEM((6 * states, 2 * states * LANES), jnp.bfloat16),
            pltpu.VMEM((chunk * max(rows), 2 * states * LANES), jnp.float32),
            pltpu.VMEM((states * halves, max(rows), LANES), jnp.float32),
            *pair(lambda n, t, c, r: (n + 2, t + 16, inner_width)),
            *pair(lambda n, t, c, r: (n, t, inner_width)),
            *pair(lambda n, t, c, r: (c, t * r, LANES)),
            *pair(lambda n, t, c, r: (c, t * r, LANES)),
            *pair(lambda n, t, c, r: (t * r, LANES)),
            *pair(lambda n, t, c, r: (c, states * r, LANES)),
            *pair(lambda n, t, c, r: (2 * c, t * r, LANES)),
        ],
        compiler_params=pltpu.CompilerParams(vmem_limit_bytes=40 * 2**20),
    )(*args)


def on_device(
    features,
    scene_codes,
    norm_gain,
    in_weight,
    conv_weight,
    conv_bias,
    proj_weight,
    step_weight,
    step_bias,
    code_table,
    decay_rates,
    skip_gain,
    out_gain,
    out_weight,
):
    nx, ny = lax.axis_size("gx"), lax.axis_size("gy")
    rows, cols, width = features.shape
    inner_width = in_weight.shape[1] // 2
    states = decay_rates.shape[1]
    rp, cp = rows // nx, cols // ny
    codes = scene_codes.astype(jnp.bfloat16)

    def payload(block, code):
        lines, length, _ = block.shape
        size = -(-(length + 1) // 16) * 16
        code = jnp.pad(code[:, None, :], ((0, 0), (0, size - length - 1), (0, width - length)))
        return jnp.concatenate([block, code], axis=1)

    row_load = payload(features, codes)
    col_load = payload(jnp.swapaxes(features, 0, 1), codes.T)
    row_size, col_size = row_load.shape[1], col_load.shape[1]
    edges = tuple(jnp.stack([load[0], load[-1]]) for load in (row_load, col_load))
    row_load, col_load = (jnp.pad(load, ((1, 1), (0, 0), (0, 0))) for load in (row_load, col_load))
    xr = jnp.stack([row_load[k * rp : k * rp + rp + 2] for k in range(nx)])
    xc = jnp.stack([col_load[k * cp : k * cp + cp + 2] for k in range(ny)])
    got_r, got_c, halo_r, halo_c = exchange(
        xr.reshape(nx, (rp + 2) * row_size, width),
        xc.reshape(ny, (cp + 2) * col_size, width),
        0,
        edges,
    )
    place_x, place_y = lax.axis_index("gx"), lax.axis_index("gy")

    def assembled(got, halo, parts, lines, size, length, inner, outer, inner_count, outer_count):
        got = got.reshape(parts, lines + 2, size, width)
        code = got[:, 1:-1, length, :length].transpose(1, 0, 2).reshape(lines, parts * length)
        feats = got[:, :, :length].transpose(1, 0, 2, 3)
        none = jnp.zeros_like(feats[0])
        halo = halo.reshape(2, parts, size, width)
        before = jnp.where(outer > 0, halo[0, :, :length], none)
        after = jnp.where(outer < outer_count - 1, halo[1, :, :length], none)
        feats = jnp.concatenate(
            [
                jnp.where(inner == 0, before, feats[0])[None],
                feats[1:-1],
                jnp.where(inner == inner_count - 1, after, feats[-1])[None],
            ]
        )
        return feats.reshape(lines + 2, parts * length, width), code.astype(jnp.int32)

    low_rank = step_weight.shape[1]
    proj = proj_weight.reshape(inner_width, -1, low_rank + 2 * states)
    proj = jnp.concatenate([proj[..., low_rank:], proj[..., :low_rank]], axis=-1)
    proj = jnp.pad(proj, ((0, 0), (0, 0), (0, LANES - low_rank - 2 * states)))
    weights = (
        norm_gain[None, :], in_weight, conv_weight.reshape(9, inner_width), conv_bias[None, :],
        proj.reshape(inner_width, -1), step_weight, step_bias, code_table, decay_rates, skip_gain,
    )
    feats_r, codes_r = assembled(
        got_r, halo_r, nx, rp, row_size, cols, place_x, place_y, nx, ny
    )
    feats_c, codes_c = assembled(
        got_c, halo_c, ny, cp, col_size, rows, place_y, place_x, ny, nx
    )
    y_r, y_c = strips(
        feats_r, codes_r.reshape(-1, 1), feats_c, codes_c.reshape(-1, 1), weights, states, low_rank
    )
    y_r = y_r.reshape(rp, nx, cols, inner_width).transpose(1, 0, 2, 3)
    y_c = y_c.reshape(cp, ny, rows, inner_width).transpose(1, 0, 2, 3)
    back_r, back_c = exchange(
        y_r.reshape(nx, rp * cols, inner_width), y_c.reshape(ny, cp * rows, inner_width), 1
    )
    back_r = back_r.astype(jnp.float32).reshape(rows, cols, inner_width)
    back_c = back_c.astype(jnp.float32).reshape(cols, rows, inner_width)
    total = back_r + jnp.swapaxes(back_c, 0, 1)

    source = features.astype(jnp.float32)
    normed = layer_norm(source, norm_gain).astype(jnp.bfloat16)
    gate = jnp.dot(
        normed.reshape(-1, width), in_weight[:, inner_width:], preferred_element_type=jnp.float32
    ).astype(jnp.bfloat16).reshape(rows, cols, inner_width)
    normed_out = layer_norm(total, out_gain)
    mixed = (normed_out * jax.nn.silu(gate.astype(jnp.float32))).astype(jnp.bfloat16)
    added = jnp.dot(
        mixed.reshape(-1, inner_width), out_weight, preferred_element_type=jnp.float32
    ).reshape(rows, cols, width)
    return (source + added).astype(jnp.bfloat16)


def solution(mesh):
    placed = (P(("groups", "gy"), "gx", None), P(("groups", "gy"), "gx")) + (P(),) * 12
    return jax.shard_map(
        on_device,
        mesh=mesh,
        in_specs=placed,
        out_specs=P(("groups", "gy"), "gx", None),
        check_vma=False,
    )
```

```python
import functools
import math

import jax
import jax.numpy as jnp
from jax import lax
from jax.experimental import pallas as pl
from jax.experimental.pallas import tpu as pltpu
from jax.sharding import PartitionSpec as P

MESH = pl.DeviceIdType.MESH
LANES = 128


def layer_norm(values, gain):
    mean = jnp.mean(values, axis=-1, keepdims=True)
    centered = values - mean
    spread = jnp.mean(centered * centered, axis=-1, keepdims=True)
    return centered * lax.rsqrt(spread + 1e-05) * gain


def exchange_kernel(nx, ny, halo, *refs):
    refs = list(refs)
    take = lambda count: [refs.pop(0) for _ in range(count)]
    xr, xc = take(2)
    edge_r, edge_c = take(2) if halo else (None, None)
    out_r, out_c = take(2)
    halo_r, halo_c = take(2) if halo else (None, None)
    send_r, recv_r, send_c, recv_c, own_sem = take(5)
    edge_sem, halo_r_sem, halo_c_sem = take(3) if halo else (None,) * 3
    group = lax.axis_index("groups")
    row = lax.axis_index("gy")
    col = lax.axis_index("gx")
    barrier = pltpu.get_barrier_semaphore()
    inside_up, inside_down = row > 0, row < ny - 1
    inside_left, inside_right = col > 0, col < nx - 1

    def greet(to_row, to_col):
        pl.semaphore_signal(barrier, inc=1, device_id=(group, to_row, to_col), device_id_type=MESH)

    for k in range(1, nx):
        greet(row, lax.rem(col + k, nx))
    for k in range(1, ny):
        greet(lax.rem(row + k, ny), col)
    if halo:
        receives = (
            (inside_up & (col == 0), [(lax.rem(row + ny - 1, ny), s) for s in range(nx)]),
            (inside_down & (col == nx - 1), [(lax.rem(row + 1, ny), s) for s in range(nx)]),
            (inside_left & (row == 0), [(s, lax.rem(col + nx - 1, nx)) for s in range(ny)]),
            (inside_right & (row == ny - 1), [(s, lax.rem(col + 1, nx)) for s in range(ny)]),
        )
        for here, sources in receives:

            @pl.when(here)
            def _(sources=sources):
                for source in sources:
                    greet(*source)

    own_r = pltpu.make_async_copy(xr.at[col], out_r.at[col], own_sem.at[0])
    own_c = pltpu.make_async_copy(xc.at[row], out_c.at[row], own_sem.at[1])
    own_r.start()
    own_c.start()
    peers = nx + ny - 2
    if halo:
        peers += lax.div(row + ny - 1, ny) + 1 - lax.div(row + 1, ny)
        peers += lax.div(col + nx - 1, nx) + 1 - lax.div(col + 1, nx)
    pl.semaphore_wait(barrier, peers)
    copies = []
    if halo:
        def edge(which, slot):
            down = which % 2 == 0
            if which < 2:
                return pltpu.make_async_remote_copy(
                    src_ref=edge_r.at[1 if down else 0],
                    dst_ref=halo_r.at[which * nx + slot],
                    send_sem=edge_sem.at[which],
                    recv_sem=halo_r_sem.at[which * nx + slot],
                    device_id=(group, lax.rem(row + (1 if down else ny - 1), ny), 0 if down else nx - 1),
                    device_id_type=MESH,
                )
            return pltpu.make_async_remote_copy(
                src_ref=edge_c.at[1 if down else 0],
                dst_ref=halo_c.at[(which - 2) * ny + slot],
                send_sem=edge_sem.at[which],
                recv_sem=halo_c_sem.at[(which - 2) * ny + slot],
                device_id=(group, 0 if down else ny - 1, lax.rem(col + (1 if down else nx - 1), nx)),
                device_id_type=MESH,
            )

        sends = (inside_down, inside_up, inside_right, inside_left)
        for which in range(4):

            @pl.when(sends[which])
            def _(which=which):
                edge(which, col if which < 2 else row).start()

    for k in range(1, ny):
        to = lax.rem(row + k, ny)
        copies.append(
            pltpu.make_async_remote_copy(
                src_ref=xc.at[to],
                dst_ref=out_c.at[row],
                send_sem=send_c.at[k - 1],
                recv_sem=recv_c.at[k - 1],
                device_id=(group, to, col),
                device_id_type=MESH,
            )
        )
        copies[-1].start()
    for k in range(1, nx):
        to = lax.rem(col + k, nx)
        copies.append(
            pltpu.make_async_remote_copy(
                src_ref=xr.at[to],
                dst_ref=out_r.at[col],
                send_sem=send_r.at[k - 1],
                recv_sem=recv_r.at[k - 1],
                device_id=(group, row, to),
                device_id_type=MESH,
            )
        )
        copies[-1].start()
    own_r.wait()
    own_c.wait()
    for copy in copies:
        copy.wait()
    if halo:
        for which in range(4):

            @pl.when(sends[which])
            def _(which=which):
                edge(which, col if which < 2 else row).wait_send()

            @pl.when(receives[which][0])
            def _(which=which):
                for slot in range(nx if which < 2 else ny):
                    edge(which, slot).wait_recv()


def exchange(xr, xc, call, edges=None):
    nx, ny = xr.shape[0], xc.shape[0]
    shapes = [xr.shape, xc.shape]
    sems = [(nx - 1,), (nx - 1,), (ny - 1,), (ny - 1,), (2,)]
    args = [xr, xc]
    if edges is not None:
        args += list(edges)
        shapes += [(2 * nx,) + edges[0].shape[1:], (2 * ny,) + edges[1].shape[1:]]
        sems += [(4,), (2 * nx,), (2 * ny,)]
    return pl.pallas_call(
        functools.partial(exchange_kernel, nx, ny, edges is not None),
        out_shape=tuple(jax.ShapeDtypeStruct(shape, xr.dtype) for shape in shapes),
        in_specs=[pl.BlockSpec(memory_space=pltpu.VMEM)] * len(args),
        out_specs=(pl.BlockSpec(memory_space=pltpu.VMEM),) * len(shapes),
        scratch_shapes=[pltpu.SemaphoreType.DMA(shape) for shape in sems],
        compiler_params=pltpu.CompilerParams(
            collective_id=call, has_side_effects=True, vmem_limit_bytes=16 * 2**20
        ),
    )(*args)


def to_eight(count):
    return -(-count // 8) * 8


def chosen(picks, values):
    high = values.astype(jnp.bfloat16)
    rest = values - high.astype(jnp.float32)
    middle = rest.astype(jnp.bfloat16)
    low = (rest - middle.astype(jnp.float32)).astype(jnp.bfloat16)
    out = [jnp.dot(picks, part, preferred_element_type=jnp.float32) for part in (low, middle, high)]
    return (out[0] + out[1]) + out[2]


def strip_kernel(
    states, low_rank, chunk,
    feats_r, codes_r, feats_c, codes_c,
    norm_gain, in_weight, conv_weight, conv_bias, proj, step_weight, step_bias, code_table,
    decay_rates, skip_gain,
    y_r, y_c,
    pick, wide, state_ref, inner_r, inner_c, sig_r, sig_c, step_r, step_c, drive_r, drive_c,
    coef_r, coef_c, rate_r, rate_c, out_r, out_c,
):
    place = lax.broadcasted_iota(jnp.int32, pick.shape, 0)
    lane = lax.broadcasted_iota(jnp.int32, pick.shape, 1)
    pick[...] = jnp.where(lax.rem(place, 2 * states) == lane // LANES, 1.0, 0.0).astype(jnp.bfloat16)
    inner_width = code_table.shape[1]
    halves = inner_width // LANES
    exact = lax.Precision.HIGHEST

    def run(feats, codes, inner_ref, sig, step, drive, coef, rate, out, y, first):
        lines, length = feats.shape[0] - 2, feats.shape[1]
        copies = step.shape[0]
        inside = halves // copies
        used = inside * 2 * lines
        rows = step.shape[1] // length
        if used < rows:
            for ref in (step, drive, coef, rate):
                ref[...] = jnp.zeros_like(ref)
        inner_ref[:, :8, :] = jnp.zeros((lines + 2, 8, inner_width), jnp.float32)
        inner_ref[:, 8 + length :, :] = jnp.zeros((lines + 2, 8, inner_width), jnp.float32)
        for line in range(lines + 2):
            normed = layer_norm(feats[line].astype(jnp.float32), norm_gain[...])
            inner = jnp.dot(
                normed.astype(jnp.bfloat16),
                in_weight[:, :inner_width],
                preferred_element_type=jnp.float32,
            )
            inner_ref[line, 8 : 8 + length, :] = inner.astype(jnp.bfloat16).astype(jnp.float32)
        at_row = lax.broadcasted_iota(jnp.int32, (length, length), 0)
        at_col = lax.broadcasted_iota(jnp.int32, (length, length), 1)
        turn = jnp.where(at_row + at_col == length - 1, 1.0, 0.0).astype(jnp.bfloat16)
        hot = codes[...] == lax.broadcasted_iota(
            jnp.int32, (lines * length, code_table.shape[0]), 1
        )
        all_offsets = chosen(jnp.where(hot, 1.0, 0.0).astype(jnp.bfloat16), code_table[...])
        slot_at = lax.broadcasted_iota(jnp.int32, (rows, LANES), 0)
        ahead = lax.rem(slot_at // lines, 2) == 0

        def slots(line, d, half):
            part, inner_half = half % copies, half // copies
            return part, (inner_half * 2 + d) * lines + line

        for d in range(2):
            for half in range(halves):
                for line in range(lines):
                    part, slot = slots(line, d, half)
                    rate[part, pl.ds(slot, states, stride=rows), :] = decay_rates[
                        first + d, :, half * LANES : (half + 1) * LANES
                    ] * (-1.0 / math.log(2.0))
        for line in range(lines):
            summed = jnp.zeros((length, inner_width), jnp.float32) + conv_bias[...]
            for i in range(3):
                for j in range(3):
                    tap = i * 3 + j if first == 0 else j * 3 + i
                    summed = summed + (
                        inner_ref[line + i, 7 + j : 7 + j + length, :] * conv_weight[tap : tap + 1, :]
                    )
            signal_low = jax.nn.silu(summed).astype(jnp.bfloat16)
            signal = signal_low.astype(jnp.float32)
            sig[line] = signal
            offsets = all_offsets[line * length : (line + 1) * length, :]
            for d in range(2):
                way = first + d
                mix = jnp.dot(
                    signal_low,
                    proj[:, way * LANES : (way + 1) * LANES],
                    preferred_element_type=jnp.float32,
                )
                raw = (
                    jnp.dot(
                        mix[:, 2 * states : 2 * states + low_rank],
                        step_weight[way],
                        precision=exact,
                        preferred_element_type=jnp.float32,
                    )
                    + step_bias[way : way + 1, :]
                    + offsets
                )
                size = jnp.maximum(raw, 0.0) + jnp.log1p(jnp.exp(-jnp.abs(raw)))
                push = size * signal
                if d == 1:
                    mix = chosen(turn, mix)
                for half in range(halves):
                    part, slot = slots(line, d, half)
                    at = pl.ds(slot, length, stride=rows)
                    step[part, at, :] = size[:, half * LANES : (half + 1) * LANES]
                    drive[part, at, :] = push[:, half * LANES : (half + 1) * LANES]
                    if part == 0:
                        coef[at, :] = mix

        state_ref[...] = jnp.zeros_like(state_ref)

        @pl.loop(0, length // chunk)
        def _(block):
            span = chunk * rows
            values = coef[pl.ds(pl.multiple_of(block * span, span), span), :][:, : 2 * states]
            high = values.astype(jnp.bfloat16)
            rest = values - high.astype(jnp.float32)
            middle = rest.astype(jnp.bfloat16)
            low = (rest - middle.astype(jnp.float32)).astype(jnp.bfloat16)
            parts = jnp.concatenate([high, middle, low], axis=1)
            wide[:span, :] = jnp.dot(parts, pick[...], preferred_element_type=jnp.float32)

            def advance(k, state):
                at = pl.ds(pl.multiple_of(k * rows, rows), rows)
                now_at = pl.ds(pl.multiple_of((block * chunk + k) * rows, rows), rows)
                last_at = pl.ds(
                    pl.multiple_of((length - 1 - block * chunk - k) * rows, rows), rows
                )
                size, push = (
                    [jnp.where(ahead, ref[p, now_at, :], ref[p, last_at, :]) for p in range(copies)]
                    for ref in (step, drive)
                )
                new = []
                sums = [[None, None] for _ in range(copies)]
                for n in range(states):
                    into = wide[at, n * LANES : (n + 1) * LANES]
                    outof = wide[at, (states + n) * LANES : (states + n + 1) * LANES]
                    for p in range(copies):
                        decay = jnp.exp2(size[p] * rate[p, n * rows : (n + 1) * rows, :])
                        now = decay * state[n * copies + p] + push[p] * into
                        new.append(now)
                        term = now * outof
                        old = sums[p][n % 2]
                        sums[p][n % 2] = term if old is None else old + term
                for p in range(copies):
                    out[p, now_at, :] = sums[p][0] + sums[p][1]
                    out[copies + p, last_at, :] = sums[p][0] + sums[p][1]
                return tuple(new)

            start = tuple(state_ref[k, :rows, :] for k in range(states * copies))
            end = lax.fori_loop(0, chunk, advance, start, unroll=4)
            for k in range(states * copies):
                state_ref[k, :rows, :] = end[k]

        direct = skip_gain[first : first + 1, :] + skip_gain[first + 1 : first + 2, :]
        for line in range(lines):
            for half in range(halves):
                lanes = slice(half * LANES, (half + 1) * LANES)
                part, slot = slots(line, 0, half)
                forward = out[part, pl.ds(slot, length, stride=rows), :]
                part, slot = slots(line, 1, half)
                back = out[copies + part, pl.ds(slot, length, stride=rows), :]
                total = forward + back + direct[:, lanes] * sig[line, :, lanes]
                y[line, :, lanes] = total.astype(jnp.bfloat16)

    run(feats_r, codes_r, inner_r, sig_r, step_r, drive_r, coef_r, rate_r, out_r, y_r, 0)
    run(feats_c, codes_c, inner_c, sig_c, step_c, drive_c, coef_c, rate_c, out_c, y_c, 2)


def strips(feats_r, codes_r, feats_c, codes_c, weights, states, low_rank):
    inner_width = weights[1].shape[1] // 2
    halves = inner_width // LANES
    lengths = [feats_r.shape[1], feats_c.shape[1]]
    lines = [feats_r.shape[0] - 2, feats_c.shape[0] - 2]
    copies = [1, halves]
    rows = [to_eight(halves // c * 2 * n) for c, n in zip(copies, lines)]
    chunk = math.gcd(16, math.gcd(*lengths))

    def pair(shape):
        return [pltpu.VMEM(shape(lines[k], lengths[k], copies[k], rows[k]), jnp.float32) for k in (0, 1)]

    args = (feats_r, codes_r, feats_c, codes_c) + weights
    return pl.pallas_call(
        functools.partial(strip_kernel, states, low_rank, chunk),
        out_shape=tuple(
            jax.ShapeDtypeStruct((lines[k], lengths[k], inner_width), jnp.bfloat16) for k in (0, 1)
        ),
        in_specs=[pl.BlockSpec(memory_space=pltpu.VMEM)] * len(args),
        out_specs=(pl.BlockSpec(memory_space=pltpu.VMEM),) * 2,
        scratch_shapes=[
            pltpu.VMEM((6 * states, 2 * states * LANES), jnp.bfloat16),
            pltpu.VMEM((chunk * max(rows), 2 * states * LANES), jnp.float32),
            pltpu.VMEM((states * halves, max(rows), LANES), jnp.float32),
            *pair(lambda n, t, c, r: (n + 2, t + 16, inner_width)),
            *pair(lambda n, t, c, r: (n, t, inner_width)),
            *pair(lambda n, t, c, r: (c, t * r, LANES)),
            *pair(lambda n, t, c, r: (c, t * r, LANES)),
            *pair(lambda n, t, c, r: (t * r, LANES)),
            *pair(lambda n, t, c, r: (c, states * r, LANES)),
            *pair(lambda n, t, c, r: (2 * c, t * r, LANES)),
        ],
        compiler_params=pltpu.CompilerParams(vmem_limit_bytes=40 * 2**20),
    )(*args)


def on_device(
    features,
    scene_codes,
    norm_gain,
    in_weight,
    conv_weight,
    conv_bias,
    proj_weight,
    step_weight,
    step_bias,
    code_table,
    decay_rates,
    skip_gain,
    out_gain,
    out_weight,
):
    nx, ny = lax.axis_size("gx"), lax.axis_size("gy")
    rows, cols, width = features.shape
    inner_width = in_weight.shape[1] // 2
    states = decay_rates.shape[1]
    rp, cp = rows // nx, cols // ny
    codes = scene_codes.astype(jnp.bfloat16)

    def to_sixteen(count):
        return -(-count // 16) * 16

    def payload(block, code, lines, parts):
        length = block.shape[1]
        padded = jnp.pad(block, ((1, 1), (0, 0), (0, 0)))
        code = jnp.pad(code, ((0, 0), (0, width - length)))
        count = (lines + 2) * length + lines
        rest = jnp.zeros((to_sixteen(count) - count, width), block.dtype)
        slots = [
            jnp.concatenate(
                [
                    padded[k * lines : (k + 1) * lines + 2].reshape(-1, width),
                    code[k * lines : (k + 1) * lines],
                    rest,
                ]
            )
            for k in range(parts)
        ]
        edge = jnp.stack([block[0], block[-1]])
        return jnp.stack(slots), jnp.pad(edge, ((0, 0), (0, to_sixteen(length) - length), (0, 0)))

    xr, edge_r = payload(features, codes, rp, nx)
    xc, edge_c = payload(jnp.swapaxes(features, 0, 1), codes.T, cp, ny)
    got_r, got_c, halo_r, halo_c = exchange(xr, xc, 0, (edge_r, edge_c))
    place_x, place_y = lax.axis_index("gx"), lax.axis_index("gy")

    def assembled(got, halo, parts, lines, length, inner, outer, inner_count, outer_count):
        count = (lines + 2) * length
        code = got[:, count : count + lines, :length]
        code = code.transpose(1, 0, 2).reshape(lines, parts * length)
        feats = got[:, :count].reshape(parts, lines + 2, length, width).transpose(1, 0, 2, 3)
        none = jnp.zeros_like(feats[0])
        halo = halo.reshape(2, parts, -1, width)
        before = jnp.where(outer > 0, halo[0, :, :length], none)
        after = jnp.where(outer < outer_count - 1, halo[1, :, :length], none)
        feats = jnp.concatenate(
            [
                jnp.where(inner == 0, before, feats[0])[None],
                feats[1:-1],
                jnp.where(inner == inner_count - 1, after, feats[-1])[None],
            ]
        )
        return feats.reshape(lines + 2, parts * length, width), code.astype(jnp.int32)

    low_rank = step_weight.shape[1]
    proj = proj_weight.reshape(inner_width, -1, low_rank + 2 * states)
    proj = jnp.concatenate([proj[..., low_rank:], proj[..., :low_rank]], axis=-1)
    proj = jnp.pad(proj, ((0, 0), (0, 0), (0, LANES - low_rank - 2 * states)))
    weights = (
        norm_gain[None, :], in_weight, conv_weight.reshape(9, inner_width), conv_bias[None, :],
        proj.reshape(inner_width, -1), step_weight, step_bias, code_table, decay_rates, skip_gain,
    )
    feats_r, codes_r = assembled(
        got_r, halo_r, nx, rp, cols, place_x, place_y, nx, ny
    )
    feats_c, codes_c = assembled(
        got_c, halo_c, ny, cp, rows, place_y, place_x, ny, nx
    )
    y_r, y_c = strips(
        feats_r, codes_r.reshape(-1, 1), feats_c, codes_c.reshape(-1, 1), weights, states, low_rank
    )
    y_r = y_r.reshape(rp, nx, cols, inner_width).transpose(1, 0, 2, 3)
    y_c = y_c.reshape(cp, ny, rows, inner_width).transpose(1, 0, 2, 3)
    back_r, back_c = exchange(
        y_r.reshape(nx, rp * cols, inner_width), y_c.reshape(ny, cp * rows, inner_width), 1
    )
    back_r = back_r.astype(jnp.float32).reshape(rows, cols, inner_width)
    back_c = back_c.astype(jnp.float32).reshape(cols, rows, inner_width)
    total = back_r + jnp.swapaxes(back_c, 0, 1)

    source = features.astype(jnp.float32)
    normed = layer_norm(source, norm_gain).astype(jnp.bfloat16)
    gate = jnp.dot(
        normed.reshape(-1, width), in_weight[:, inner_width:], preferred_element_type=jnp.float32
    ).astype(jnp.bfloat16).reshape(rows, cols, inner_width)
    normed_out = layer_norm(total, out_gain)
    mixed = (normed_out * jax.nn.silu(gate.astype(jnp.float32))).astype(jnp.bfloat16)
    added = jnp.dot(
        mixed.reshape(-1, inner_width), out_weight, preferred_element_type=jnp.float32
    ).reshape(rows, cols, width)
    return (source + added).astype(jnp.bfloat16)


def solution(mesh):
    placed = (P(("groups", "gy"), "gx", None), P(("groups", "gy"), "gx")) + (P(),) * 12
    return jax.shard_map(
        on_device,
        mesh=mesh,
        in_specs=placed,
        out_specs=P(("groups", "gy"), "gx", None),
        check_vma=False,
    )
```
